256 devices in a mesh: dp: 32 (over x, z), ctx: 8 (over y, core).
Axes of the slice: x: 4, y: 4, z: 8, core: 2. Of those that a mesh axis runs over, the one named last changes fastest.
Arguments:
- queries: bfloat16 [32, 1024, 2048], P('dp', 'ctx'), may hold values from -180 to 180
- encodings: bfloat16 [32, 32, 128, 896], P('dp', 'ctx'), may hold values from -6 to 6
- key_value_weight: bfloat16 [4096, 896], P('dp'), may hold values from -0.1875 to 0.1875
- neighbour_shard: int32 [32, 16, 2], P('dp', 'ctx'), may hold values from 0 to 7, as said below
- neighbour_row: int32 [32, 16, 2], P('dp', 'ctx'), may hold values from 0 to 3
- pad_count: int32 [32, 16, 2], P('dp', 'ctx'), may hold values from 0 to 96
- attended_cotangent: bfloat16 [32, 1024, 2048], P('dp', 'ctx'), may hold values from -6 to 6
Outputs:
- attended: bfloat16 [32, 1024, 2048], P('dp', 'ctx')
- query_gradient: bfloat16 [32, 1024, 2048], P('dp', 'ctx')
- encoding_gradient: bfloat16 [32, 32, 128, 896], P('dp', 'ctx')
- weight_gradient: float32 [4096, 896], P('dp')
The draws below stay inside these ranges and needn't reach their ends.
Inputs may be any that keep to these rules, and one draw needn't show every extreme that they name: `neighbour_shard`: take a sequence's groups in blocks of 2 in order: the rows that one block names on one owner are distinct, at most 2 slots of a block name one owner, and in each sequence one owner drawn from the seed is named by exactly 2 slots of every block.
All inputs are finite; a program needn't handle non-finite values.
Results may differ from the reference program's by a relative error of at most 0.022.
Values may be sent and summed in bfloat16 or wider, within the bound.
No kernel may reach another device: no remote copies, remote signals or barrier semaphores. Data moves between devices by JAX's collectives and lax.ppermute only.
A program may use at most 128 MiB of HBM per device.

```python
import jax
import jax.numpy as jnp
from jax import lax

HEADS = 16
HD = 128
ENC_D = 896
NBL = 128
GROUP = 64
NB = 2
PADMAX = 96
HQ = 2048
REQ_DEV = 4
ENC_DEV = 4
CAP = 2
GROUPS = 16
SEQ = 1024
ENC_ROWS = 32
BATCH = 32
N_CTX = 8


def neighbour_lists(key):
    hot_owner = jax.random.randint(jax.random.fold_in(key, 11), (BATCH,), 0, N_CTX)
    device_keys = jax.random.split(jax.random.fold_in(key, 12), BATCH * N_CTX)

    def one_device(device_key, hot_index):
        key_order, key_hot, key_other, key_owner = jax.random.split(device_key, 4)
        slot_order = jax.random.permutation(key_order, REQ_DEV)
        hot_rows = jax.random.permutation(key_hot, ENC_DEV)[:CAP]
        other_rows = jax.random.permutation(key_other, ENC_DEV)[:REQ_DEV - CAP]
        other_owner = (hot_index + 1 + jax.random.randint(key_owner, (REQ_DEV - CAP,), 0, N_CTX - 1)) % N_CTX
        owners = jnp.concatenate([jnp.full((CAP,), hot_index, jnp.int32), other_owner.astype(jnp.int32)])
        rows_all = jnp.concatenate([hot_rows, other_rows]).astype(jnp.int32)
        return (owners[slot_order], rows_all[slot_order])
    owners, rows_all = jax.vmap(one_device)(device_keys, jnp.repeat(hot_owner, N_CTX))
    return (owners.reshape(BATCH, GROUPS, NB), rows_all.reshape(BATCH, GROUPS, NB))


def draw_neighbour_shard(key, part):
    return neighbour_lists(key)[0]


def draw_neighbour_row(key, part):
    return neighbour_lists(key)[1]


def draw_queries(key, part):
    key = jax.random.fold_in(key, 5)
    key_base = jax.random.fold_in(key, 0)
    draw_shape = (BATCH, SEQ, HQ)
    values = jnp.clip(jax.random.normal(key_base, draw_shape, jnp.float32), -6.0, 6.0)
    return values.astype(jnp.bfloat16)


def draw_attended_cotangent(key, part):
    key = jax.random.fold_in(key, 6)
    values = jnp.clip(jax.random.normal(key, (BATCH, SEQ, HQ), jnp.float32), -6.0, 6.0)
    return values.astype(jnp.bfloat16)


def set_ends(values, key, smallest, top_value):
    longest = values.shape.index(max(values.shape))
    spots = []
    for shift in (0, 1):
        where = [jax.random.randint(jax.random.fold_in(key, axis), (), 0, length) for axis, length in enumerate(values.shape)]
        where[longest] = (where[longest] + shift) % values.shape[longest]
        spots.append(tuple(where))
    return values.at[spots[0]].set(smallest).at[spots[1]].set(top_value)


def block_levels(stream_key, extent, pieces, least, top_value):
    def one(dim, shards_of):
        steps = jax.random.uniform(jax.random.fold_in(jax.random.fold_in(stream_key, 6), dim), (shards_of,), jnp.float32, least / len(pieces), top_value / len(pieces))
        return jnp.repeat(jnp.exp(steps), extent[dim] // shards_of).reshape((-1,) + (1,) * (len(extent) - dim - 1))

    loudness = one(*pieces[0])
    for cut in pieces[1:]:
        loudness = loudness * one(*cut)
    return loudness


def gaussian(rng, extent, scale, limit, cuts=(), held_as=jnp.bfloat16):
    values = scale * jax.random.normal(rng, extent, jnp.float32)
    if cuts:
        values = values * block_levels(rng, extent, cuts, -0.22, 0.18)
    return jnp.clip(values, -limit, limit).astype(held_as)


def setup_inputs(seed: int = 0) -> dict:
    seeds = jax.random.split(jax.random.key(seed), 8)
    return {
        "queries": draw_queries(jax.random.fold_in(seeds[7], 71), 0),
        "encodings": gaussian(seeds[1], (BATCH, ENC_ROWS, NBL, ENC_D), 1.0, 6.0, ((0, 32), (1, 8))),
        "key_value_weight": gaussian(seeds[2], (2 * HQ, ENC_D), ENC_D ** -0.5, 0.1875, ((0, 32),)),
        "neighbour_shard": draw_neighbour_shard(jax.random.fold_in(seeds[7], 71), 0),
        "neighbour_row": draw_neighbour_row(jax.random.fold_in(seeds[7], 71), 0),
        "pad_count": set_ends(jax.random.randint(seeds[5], (BATCH, GROUPS, NB), 0, PADMAX + 1), jax.random.fold_in(seeds[5], 1), 0, PADMAX).astype(jnp.int32),
        "attended_cotangent": draw_attended_cotangent(jax.random.fold_in(seeds[7], 71), 0),
    }


neg_fill = -1e30


def group_math(query_block, key_value_block, pad_block, cotangent_block):
    groups = query_block.shape[0]
    keys_total = key_value_block.shape[1]
    score_scale = HD ** -0.5
    query_heads = query_block.reshape(groups, GROUP, HEADS, HD).astype(jnp.float32)
    key_heads = key_value_block[:, :, :HQ].reshape(groups, keys_total, HEADS, HD).astype(jnp.float32)
    value_heads = key_value_block[:, :, HQ:].reshape(groups, keys_total, HEADS, HD).astype(jnp.float32)
    cotangent = cotangent_block.reshape(groups, GROUP, HEADS, HD).astype(jnp.float32)
    scores = jnp.einsum('clhd,cjhd->chlj', query_heads, key_heads) * score_scale
    position = jnp.arange(keys_total, dtype=jnp.int32) % NBL
    slot_of_key = jnp.arange(keys_total, dtype=jnp.int32) // NBL
    live_count = NBL - pad_block[:, slot_of_key]
    is_live = position[None, :] < live_count
    scores = jnp.where(is_live[:, None, None, :], scores, neg_fill)
    row_max = jnp.max(scores, axis=-1, keepdims=True)
    exponent = jnp.exp(scores - row_max)
    probabilities = exponent / jnp.sum(exponent, axis=-1, keepdims=True)
    probs_low = lax.optimization_barrier(probabilities.astype(jnp.bfloat16))
    attended = jnp.einsum('chlj,cjhd->clhd', probs_low.astype(jnp.float32), value_heads).astype(jnp.bfloat16)
    dprob = jnp.einsum('clhd,cjhd->chlj', cotangent, value_heads)
    row_delta = jnp.sum(probabilities * dprob, axis=-1, keepdims=True)
    dscore = lax.optimization_barrier((probabilities * (dprob - row_delta) * score_scale).astype(jnp.bfloat16))
    query_grad = jnp.einsum('chlj,cjhd->clhd', dscore.astype(jnp.float32), key_heads).astype(jnp.bfloat16)
    key_grad = jnp.einsum('chlj,clhd->cjhd', dscore.astype(jnp.float32), query_heads).astype(jnp.bfloat16)
    value_grad = jnp.einsum('chlj,clhd->cjhd', probs_low.astype(jnp.float32), cotangent).astype(jnp.bfloat16)
    key_value_grad = jnp.concatenate([key_grad.reshape(groups, keys_total, HQ), value_grad.reshape(groups, keys_total, HQ)], axis=-1)
    return attended.reshape(groups * GROUP, HQ), query_grad.reshape(groups * GROUP, HQ), key_value_grad


def reference(queries, encodings, key_value_weight, neighbour_shard, neighbour_row, pad_count, attended_cotangent):
    def one_sequence(running, sequence_items):
        query_seq, encoding_seq, shard_seq, row_seq, pad_seq, cotangent_seq = sequence_items
        row_ids = (shard_seq * ENC_DEV + row_seq).reshape(GROUPS * NB).astype(jnp.int32)
        fetched = encoding_seq[row_ids]
        flat_rows = fetched.reshape(GROUPS * NB * NBL, ENC_D)
        key_values = jnp.dot(flat_rows, key_value_weight.T, preferred_element_type=jnp.float32).astype(jnp.bfloat16)
        key_values = lax.optimization_barrier(key_values)
        attended, query_grad, key_value_grad = group_math(
            query_seq.reshape(GROUPS, GROUP, HQ),
            key_values.reshape(GROUPS, NB * NBL, 2 * HQ),
            pad_seq,
            cotangent_seq.reshape(GROUPS, GROUP, HQ))
        grad_flat = key_value_grad.reshape(GROUPS * NB * NBL, 2 * HQ)
        encoding_terms = jnp.dot(grad_flat, key_value_weight, preferred_element_type=jnp.float32).astype(jnp.bfloat16)
        encoding_terms = lax.optimization_barrier(encoding_terms)
        summed = jax.ops.segment_sum(encoding_terms.reshape(GROUPS * NB, NBL * ENC_D).astype(jnp.float32), row_ids, ENC_ROWS)
        encoding_grad = summed.astype(jnp.bfloat16).reshape(ENC_ROWS, NBL, ENC_D)
        grad_blocks = grad_flat.reshape(N_CTX, REQ_DEV * NBL, 2 * HQ)
        row_blocks = flat_rows.reshape(N_CTX, REQ_DEV * NBL, ENC_D)

        def block_term(total, pair_items):
            grad_part, row_part = pair_items
            product = lax.dot_general(grad_part, row_part, (((0,), (0,)), ((), ())), preferred_element_type=jnp.float32)
            rounded = lax.optimization_barrier(product.astype(jnp.bfloat16))
            return total + rounded.astype(jnp.float32), None

        running, _ = lax.scan(block_term, running, (grad_blocks, row_blocks))
        return running, (attended, query_grad, encoding_grad)

    initial = jnp.zeros((2 * HQ, ENC_D), jnp.float32)
    weight_gradient, outputs = lax.scan(one_sequence, initial, (queries, encodings, neighbour_shard, neighbour_row, pad_count, attended_cotangent))
    attended, query_gradient, encoding_gradient = outputs
    return attended, query_gradient, encoding_gradient, weight_gradient
```

```python
import functools

import jax
import jax.numpy as jnp
from jax import lax
from jax.experimental import pallas as pl
from jax.experimental.pallas import tpu as pltpu
from jax.sharding import PartitionSpec as P

HEADS = 16
HD = 128
ENC_D = 896
NBL = 128
GROUP = 64
HQ = 2048
NX, NY, NZ = 4, 4, 8
SLOTS = 8
NEG = -1e30
BF = jnp.bfloat16
F32 = jnp.float32
AXES = ("dp", "ctx")


def _lin(x, y, z, c):
    return ((x % NX) * NZ + z % NZ) * (NY * 2) + (y % NY) * 2 + c


def _pairs(move):
    return [
        (_lin(x, y, z, c), _lin(*move(x, y, z, c)))
        for x in range(NX)
        for z in range(NZ)
        for y in range(NY)
        for c in range(2)
    ]


Y_UP = _pairs(lambda x, y, z, c: (x, y + 1, z, c))
Y_DN = _pairs(lambda x, y, z, c: (x, y - 1, z, c))
Y_TWO = _pairs(lambda x, y, z, c: (x, y + 2, z, c))
X_UP = _pairs(lambda x, y, z, c: (x + 1, y, z, c))
X_DN = _pairs(lambda x, y, z, c: (x - 1, y, z, c))
SWAP = _pairs(lambda x, y, z, c: (x, y, z, 1 - c))
Z_FIRST = _pairs(lambda x, y, z, c: (x, y, z - c, c))
Z_STEP = _pairs(lambda x, y, z, c: (x, y, z + 1 - 2 * c, c))
Z_FIRST_BACK = _pairs(lambda x, y, z, c: (x, y, z + c, c))
Z_STEP_BACK = _pairs(lambda x, y, z, c: (x, y, z - 1 + 2 * c, c))


def send(value, pairs):
    return lax.ppermute(value, AXES, pairs)


def column_of(z, c, j):
    return lax.rem(jnp.where(c == 0, z + NZ - j, z + 1 + j), NZ)


ANY = pl.BlockSpec(memory_space=pl.ANY)
VMEM = pl.BlockSpec(memory_space=pltpu.VMEM)


def params(mib):
    return pltpu.CompilerParams(vmem_limit_bytes=mib * 1024 * 1024)


def dot(a, b, dims):
    return lax.dot_general(a, b, (dims, ((), ())), preferred_element_type=F32)


def attention_kernel(
    pos, ids, pids,
    own, up, dn, far_a, far_b, p_own, p_up, p_dn, p_far_a, p_far_b,
    u0, u1, u2, u3, wup_a, wup_b, wdn_a, wdn_b, wfar_a, wfar_b,
    q_own, q_par, c_own, c_par,
    terms_out, grad_out, rows_out, att_own, att_par, dq_own, dq_par,
    rows, weight, qs, cs, kv, grad, terms, att, dq,
    row_sem, w_sem, q_sem, out_sem, big_sem,
):
    x, y, z, c = pos[0], pos[1], pos[2], pos[3]

    def slot_value(which, s):
        mine = ids[which * 4 + lax.rem(s, 4)]
        other = pids[which * 4 + lax.rem(s, 4)]
        return jnp.where(s < 4, mine, other)

    def fetch(s, carry):
        owner = slot_value(0, s)
        row = slot_value(1, s)
        away = lax.rem(owner // 2 + NY - y, NY)
        other = lax.rem(owner, 2) != c
        for side, bufs in enumerate(((own, up, dn, far_a, far_b), (p_own, p_up, p_dn, p_far_a, p_far_b))):
            here = other if side else jnp.logical_not(other)
            b_own, b_up, b_dn, b_fa, b_fb = bufs
            cases = (
                (away == 0, b_own, row),
                (away == NY - 1, b_up, row),
                (away == 1, b_dn, row),
                (jnp.logical_and(away == 2, row < 2), b_fa, row),
                (jnp.logical_and(away == 2, row >= 2), b_fb, row - 2),
            )
            for cond, buf, index in cases:
                @pl.when(jnp.logical_and(here, cond))
                def _():
                    pltpu.make_async_copy(buf.at[index], rows.at[s], row_sem.at[s]).start()
        return carry

    lax.fori_loop(0, SLOTS, fetch, 0)
    us = (u0, u1, u2, u3)
    for j in range(4):
        for xx in range(NX):
            away = lax.rem(xx + NX - x, NX)
            half = j % 2
            cases = (
                (0, us[j]),
                (NX - 1, (wup_a, wup_b)[j // 2].at[half]),
                (1, (wdn_a, wdn_b)[j // 2].at[half]),
                (2, (wfar_a, wfar_b)[j // 2].at[half]),
            )
            for value, src in cases:
                @pl.when(away == value)
                def _():
                    pltpu.make_async_copy(src, weight.at[j, xx], w_sem.at[j]).start()
    for j in range(4):
        col = column_of(z, c, j)
        for hi in range(2):
            lanes = pl.ds(pl.multiple_of((hi * NZ + col) * HD, HD), HD)
            for part, (qr, cr) in enumerate(((q_own, c_own), (q_par, c_par))):
                here = pl.ds(part * 128, 128)
                pltpu.make_async_copy(qr.at[:, lanes], qs.at[2 * j + hi, here], q_sem).start()
                pltpu.make_async_copy(cr.at[:, lanes], cs.at[2 * j + hi, here], q_sem).start()
    pltpu.make_async_copy(qs, qs, q_sem).wait()
    pltpu.make_async_copy(cs, cs, q_sem).wait()
    for s in range(SLOTS):
        pltpu.make_async_copy(rows.at[s], rows.at[s], row_sem.at[s]).wait()
    out_rows = pltpu.make_async_copy(rows, rows_out, big_sem.at[0])
    out_rows.start()

    scale = HD ** -0.5
    lane = lax.broadcasted_iota(jnp.int32, (GROUP, 2 * NBL), 1)

    def heads(j, carry):
        pltpu.make_async_copy(weight.at[j], weight.at[j], w_sem.at[j]).wait()
        enc = rows[...].reshape(SLOTS * NBL, ENC_D)
        w = weight[j].reshape(512, ENC_D)
        kv[...] = dot(enc, w, ((1,), (1,))).astype(BF)
        for g in range(4):
            live0 = NBL - slot_value(2, 2 * g)
            live1 = NBL - slot_value(2, 2 * g + 1)
            live = lane < jnp.where(lane < NBL, live0, live1 + NBL)
            keys = pl.ds(g * 256, 256)
            for hi in range(2):
                k = kv[keys, hi * HD:(hi + 1) * HD]
                v = kv[keys, 256 + hi * HD:256 + (hi + 1) * HD]
                q = qs[2 * j + hi, g * GROUP:(g + 1) * GROUP]
                cot = cs[2 * j + hi, g * GROUP:(g + 1) * GROUP]
                s = dot(q, k, ((1,), (1,))) * scale
                s = jnp.where(live, s, NEG)
                e = jnp.exp(s - jnp.max(s, axis=1, keepdims=True))
                p = e * (1.0 / jnp.sum(e, axis=1, keepdims=True))
                pb = p.astype(BF)
                dp = dot(cot, v, ((1,), (1,)))
                delta = jnp.sum(p * dp, axis=1, keepdims=True)
                ds = (p * (dp - delta) * scale).astype(BF)
                part = g // 2
                spot = pl.ds((g % 2) * GROUP, GROUP)
                att[part, 2 * j + hi, spot] = dot(pb, v, ((1,), (0,))).astype(BF)
                dq[part, 2 * j + hi, spot] = dot(ds, k, ((1,), (0,))).astype(BF)
                grad[j, keys, hi * HD:(hi + 1) * HD] = dot(ds, q, ((0,), (0,))).astype(BF)
                grad[j, keys, 256 + hi * HD:256 + (hi + 1) * HD] = dot(pb, cot, ((0,), (0,))).astype(BF)
        pltpu.make_async_copy(grad.at[j], grad_out.at[j], out_sem.at[j]).start()
        return carry

    lax.fori_loop(0, 4, heads, 0)
    outs = [
        pltpu.make_async_copy(att.at[0], att_own, big_sem.at[1]),
        pltpu.make_async_copy(att.at[1], att_par, big_sem.at[2]),
        pltpu.make_async_copy(dq.at[0], dq_own, big_sem.at[3]),
        pltpu.make_async_copy(dq.at[1], dq_par, big_sem.at[4]),
    ]
    for copy in outs:
        copy.start()

    def back(t, carry):
        here = pl.ds(pl.multiple_of(t * 256, 256), 256)
        acc = dot(grad[0, here], weight[0].reshape(512, ENC_D), ((1,), (0,)))
        for j in range(1, 4):
            acc = acc + dot(grad[j, here], weight[j].reshape(512, ENC_D), ((1,), (0,)))
        terms[pl.ds(2 * t, 2)] = acc.astype(BF).reshape(2, NBL, ENC_D)
        return carry

    lax.fori_loop(0, 4, back, 0)
    last = pltpu.make_async_copy(terms, terms_out, big_sem.at[5])
    last.start()
    out_rows.wait()
    for copy in outs:
        copy.wait()
    for j in range(4):
        pltpu.make_async_copy(grad.at[j], grad_out.at[j], out_sem.at[j]).wait()
    last.wait()


def attention(pos, ids, pids, *arrays):
    sds = jax.ShapeDtypeStruct
    heads = sds((8, 128, HD), BF)
    return pl.pallas_call(
        attention_kernel,
        out_shape=(
            sds((SLOTS, NBL, ENC_D), BF),
            sds((4, SLOTS * NBL, 512), BF),
            sds((SLOTS, NBL, ENC_D), BF),
            heads, heads, heads, heads,
        ),
        grid_spec=pltpu.PrefetchScalarGridSpec(
            num_scalar_prefetch=3,
            grid=(),
            in_specs=[ANY] * len(arrays),
            out_specs=[ANY] * 7,
            scratch_shapes=[
                pltpu.VMEM((SLOTS, NBL, ENC_D), BF),
                pltpu.VMEM((4, NX, HD, ENC_D), BF),
                pltpu.VMEM((8, 256, HD), BF),
                pltpu.VMEM((8, 256, HD), BF),
                pltpu.VMEM((SLOTS * NBL, 512), BF),
                pltpu.VMEM((4, SLOTS * NBL, 512), BF),
                pltpu.VMEM((SLOTS, NBL, ENC_D), BF),
                pltpu.VMEM((2, 8, 128, HD), BF),
                pltpu.VMEM((2, 8, 128, HD), BF),
                pltpu.SemaphoreType.DMA((SLOTS,)),
                pltpu.SemaphoreType.DMA((4,)),
                pltpu.SemaphoreType.DMA,
                pltpu.SemaphoreType.DMA((4,)),
                pltpu.SemaphoreType.DMA((6,)),
            ],
        ),
        compiler_params=params(48),
        cost_estimate=pl.CostEstimate(flops=9_000_000_000, bytes_accessed=24_000_000, transcendentals=600_000),
        name="attention",
    )(pos, ids, pids, *arrays)


def weight_kernel(pos, grad, rows, self_out, up_a, up_b, dn_a, dn_b, far_a, far_b, parts, sem):
    x = pos[0]
    j = pl.program_id(0)
    product = dot(grad[0], rows[...].reshape(SLOTS * NBL, ENC_D), ((0,), (0,))).astype(BF)
    for xx in range(NX):
        away = lax.rem(xx + NX - x, NX)
        parts[away, j] = product[xx * HD:(xx + 1) * HD]

    @pl.when(j == 3)
    def _():
        copies = [
            pltpu.make_async_copy(parts.at[0], self_out, sem.at[0]),
            pltpu.make_async_copy(parts.at[1, 0:2], up_a, sem.at[1]),
            pltpu.make_async_copy(parts.at[1, 2:4], up_b, sem.at[2]),
            pltpu.make_async_copy(parts.at[3, 0:2], dn_a, sem.at[3]),
            pltpu.make_async_copy(parts.at[3, 2:4], dn_b, sem.at[4]),
            pltpu.make_async_copy(parts.at[2, 0:2], far_a, sem.at[5]),
            pltpu.make_async_copy(parts.at[2, 2:4], far_b, sem.at[6]),
        ]
        for copy in copies:
            copy.start()
        for copy in copies:
            copy.wait()


def weight_parts(pos, grad, rows):
    sds = jax.ShapeDtypeStruct
    pair = sds((2, HD, ENC_D), BF)
    return pl.pallas_call(
        weight_kernel,
        out_shape=(sds((4, HD, ENC_D), BF),) + (pair,) * 6,
        grid_spec=pltpu.PrefetchScalarGridSpec(
            num_scalar_prefetch=1,
            grid=(4,),
            in_specs=[
                pl.BlockSpec((1, SLOTS * NBL, 512), lambda j, p: (j, 0, 0)),
                pl.BlockSpec((SLOTS, NBL, ENC_D), lambda j, p: (0, 0, 0)),
            ],
            out_specs=[ANY] * 7,
            scratch_shapes=[pltpu.VMEM((NX, 4, HD, ENC_D), BF), pltpu.SemaphoreType.DMA((7,))],
        ),
        compiler_params=params(40),
        cost_estimate=pl.CostEstimate(flops=3_800_000_000, bytes_accessed=10_000_000, transcendentals=0),
        name="weight_parts",
    )(pos, grad, rows)


def route_kernel(pos, ids, pids, terms, p_terms, own, up_a, up_b, dn_a, dn_b, far_a, far_b, total):
    y, c = pos[1], pos[3]
    total[...] = jnp.zeros_like(total)
    for s in range(SLOTS):
        src = ids if s < 4 else pids
        owner, row = src[s % 4], src[4 + s % 4]

        @pl.when(lax.rem(owner, 2) == c)
        def _():
            place = lax.rem(owner // 2 + NY - y, NY) * 4 + row
            total[place] = total[place] + (terms[s].astype(F32) + p_terms[s ^ 4].astype(F32))

    own[...] = total[0:4].astype(BF)
    up_a[...] = total[4:6].astype(BF)
    up_b[...] = total[6:8].astype(BF)
    far_a[...] = total[8:10].astype(BF)
    far_b[...] = total[10:12].astype(BF)
    dn_a[...] = total[12:14].astype(BF)
    dn_b[...] = total[14:16].astype(BF)


def route(pos, ids, pids, terms, p_terms):
    sds = jax.ShapeDtypeStruct
    pair = sds((2, NBL, ENC_D), BF)
    return pl.pallas_call(
        route_kernel,
        out_shape=(sds((4, NBL, ENC_D), BF),) + (pair,) * 6,
        grid_spec=pltpu.PrefetchScalarGridSpec(
            num_scalar_prefetch=3,
            grid=(),
            in_specs=[VMEM] * 2,
            out_specs=[VMEM] * 7,
            scratch_shapes=[pltpu.VMEM((16, NBL, ENC_D), F32)],
        ),
        compiler_params=params(40),
        cost_estimate=pl.CostEstimate(flops=10_000_000, bytes_accessed=8_000_000, transcendentals=0),
        name="route",
    )(pos, ids, pids, terms, p_terms)


def join_kernel(pos, att_own, att_got, dq_own, dq_got, att_out, dq_out):
    z, c = pos[2], pos[3]
    for j in range(4):
        for src_core, (a, d) in ((c, (att_own, dq_own)), (1 - c, (att_got, dq_got))):
            col = column_of(z, src_core, j)
            for hi in range(2):
                lanes = pl.ds(pl.multiple_of((hi * NZ + col) * HD, HD), HD)
                att_out[:, lanes] = a[2 * j + hi]
                dq_out[:, lanes] = d[2 * j + hi]


def join(pos, *arrays):
    sds = jax.ShapeDtypeStruct
    return pl.pallas_call(
        join_kernel,
        out_shape=(sds((128, HQ), BF),) * 2,
        grid_spec=pltpu.PrefetchScalarGridSpec(
            num_scalar_prefetch=1, grid=(), in_specs=[VMEM] * 4, out_specs=[VMEM] * 2
        ),
        compiler_params=params(16),
        cost_estimate=pl.CostEstimate(flops=0, bytes_accessed=4_000_000, transcendentals=0),
        name="join",
    )(pos, *arrays)


def add(*values):
    total = values[0].astype(F32)
    for value in values[1:]:
        total = total + value.astype(F32)
    return total


def on_device(queries, encodings, weight, shard, row, pad, cotangent):
    dp, ctx = lax.axis_index("dp"), lax.axis_index("ctx")
    pos = jnp.stack([dp // NZ, ctx // 2, dp % NZ, ctx % 2]).astype(jnp.int32)
    core = ctx % 2
    ids = jnp.concatenate([shard.reshape(4), row.reshape(4), pad.reshape(4)])
    q = queries.reshape(128, HQ)
    cot = cotangent.reshape(128, HQ)
    enc = encodings.reshape(4, NBL, ENC_D)

    up = send(enc, Y_UP)
    dn = send(enc, Y_DN)
    u0 = send(weight, Z_FIRST)
    u1 = send(u0, Z_STEP)
    u2 = send(u1, Z_STEP)
    u3 = send(u2, Z_STEP)
    ua, ub = jnp.stack([u0, u1]), jnp.stack([u2, u3])
    wup_a, wdn_a = send(ua, X_UP), send(ua, X_DN)
    wup_b, wdn_b = send(ub, X_UP), send(ub, X_DN)
    wfar_a, wfar_b = send(wup_a, X_UP), send(wdn_b, X_DN)
    far_a = send(up[0:2], Y_UP)
    far_b = send(dn[2:4], Y_DN)
    pids = send(ids, SWAP)
    q_par, c_par = send(q, SWAP), send(cot, SWAP)
    p_own, p_up, p_dn = send(enc, SWAP), send(up, SWAP), send(dn, SWAP)
    p_far_a, p_far_b = send(far_a, SWAP), send(far_b, SWAP)

    terms, grad, rows, att_own, att_par, dq_own, dq_par = attention(
        pos, ids, pids,
        enc, up, dn, far_a, far_b, p_own, p_up, p_dn, p_far_a, p_far_b,
        u0, u1, u2, u3, wup_a, wup_b, wdn_a, wdn_b, wfar_a, wfar_b,
        q, q_par, cot, c_par,
    )

    p_terms = send(terms, SWAP)
    r_own, r_up_a, r_up_b, r_dn_a, r_dn_b, r_far_a, r_far_b = route(pos, ids, pids, terms, p_terms)
    s_a, s_b = send(r_far_a, Y_UP), send(r_far_b, Y_DN)
    t_up_b, t_dn_a = send(r_up_b, Y_UP), send(r_dn_a, Y_DN)
    t_up_a = send(add(r_up_a, s_a).astype(BF), Y_UP)
    t_dn_b = send(add(r_dn_b, s_b).astype(BF), Y_DN)
    enc_grad = jnp.concatenate(
        [add(r_own[0:2], t_up_a, t_dn_a).astype(BF), add(r_own[2:4], t_up_b, t_dn_b).astype(BF)]
    )

    w_self, w_up_a, w_up_b, w_dn_a, w_dn_b, w_far_a, w_far_b = weight_parts(pos, grad, rows)
    x_a, x_b = send(w_far_a, X_UP), send(w_far_b, X_DN)
    g_up_b, g_dn_a = send(w_up_b, X_UP), send(w_dn_a, X_DN)
    g_up_a = send(add(w_up_a, x_a).astype(BF), X_UP)
    g_dn_b = send(add(w_dn_b, x_b).astype(BF), X_DN)
    acc = add(w_self[3], g_up_b[1], g_dn_b[1]).astype(BF)
    acc = add(send(acc, Z_STEP_BACK), w_self[2], g_up_b[0], g_dn_b[0]).astype(BF)
    acc = add(send(acc, Z_STEP_BACK), w_self[1], g_up_a[1], g_dn_a[1]).astype(BF)
    acc = add(send(acc, Z_STEP_BACK), w_self[0], g_up_a[0], g_dn_a[0]).astype(BF)
    acc = send(acc, Z_FIRST_BACK)
    mine = lax.dynamic_slice_in_dim(acc, core * 64, 64, 0)
    other = lax.dynamic_slice_in_dim(acc, (1 - core) * 64, 64, 0)
    half = add(mine, send(other, SWAP)).astype(BF)
    half = add(half, send(half, Y_UP), send(half, Y_DN), send(half, Y_TWO))
    rest = send(half, SWAP)
    low = jnp.where(core == 0, half, rest)
    high = jnp.where(core == 0, rest, half)
    weight_gradient = jnp.concatenate([low, high])

    att, dq = join(pos, att_own, send(att_par, SWAP), dq_own, send(dq_par, SWAP))
    return (
        att.reshape(1, 128, HQ),
        dq.reshape(1, 128, HQ),
        enc_grad.reshape(1, 4, NBL, ENC_D),
        weight_gradient,
    )


def solution(mesh):
    rows = P("dp", "ctx", None)
    return jax.shard_map(
        on_device,
        mesh=mesh,
        in_specs=(rows, P("dp", "ctx", None, None), P("dp", None), rows, rows, rows, rows),
        out_specs=(rows, rows, P("dp", "ctx", None, None), P("dp", None)),
        check_vma=False,
    )
```

```python
import functools

import jax
import jax.numpy as jnp
from jax import lax
from jax.experimental import pallas as pl
from jax.experimental.pallas import tpu as pltpu
from jax.sharding import PartitionSpec as P

HEADS = 16
HD = 128
ENC_D = 896
NBL = 128
GROUP = 64
HQ = 2048
NX, NY, NZ = 4, 4, 8
SLOTS = 8
NEG = -1e30
BF = jnp.bfloat16
F32 = jnp.float32
AXES = ("dp", "ctx")


def _lin(x, y, z, c):
    return ((x % NX) * NZ + z % NZ) * (NY * 2) + (y % NY) * 2 + c


def _pairs(move):
    return [
        (_lin(x, y, z, c), _lin(*move(x, y, z, c)))
        for x in range(NX)
        for z in range(NZ)
        for y in range(NY)
        for c in range(2)
    ]


Y_UP = _pairs(lambda x, y, z, c: (x, y + 1, z, c))
Y_DN = _pairs(lambda x, y, z, c: (x, y - 1, z, c))
Y_TWO = _pairs(lambda x, y, z, c: (x, y + 2, z, c))
Y_FWD = _pairs(lambda x, y, z, c: (x, y + 1 - 2 * c, z, c))
Y_REV = _pairs(lambda x, y, z, c: (x, y - 1 + 2 * c, z, c))
X_FWD = _pairs(lambda x, y, z, c: (x + 1 - 2 * c, y, z, c))
X_REV = _pairs(lambda x, y, z, c: (x - 1 + 2 * c, y, z, c))
SWAP = _pairs(lambda x, y, z, c: (x, y, z, 1 - c))
Z_OUT = [_pairs(lambda x, y, z, c, j=j: (x, y, z + j if c == 0 else z - 1 - j, c)) for j in range(2)]
Z_BACK = [_pairs(lambda x, y, z, c, j=j: (x, y, z - j if c == 0 else z + 1 + j, c)) for j in range(2)]
Z_BACK_ACROSS = [
    _pairs(lambda x, y, z, c, j=j: (x, y, z - j if c == 0 else z + 1 + j, 1 - c)) for j in range(2)
]
Z_PAIR_OUT = _pairs(lambda x, y, z, c: (x, y, z + 2 - 4 * c, c))
Z_PAIR_BACK = _pairs(lambda x, y, z, c: (x, y, z - 2 + 4 * c, c))


def send(value, pairs):
    return lax.ppermute(value, AXES, pairs)


def column_of(z, c, j):
    return lax.rem(jnp.where(c == 0, z + NZ - j, z + 1 + j), NZ)


HBM = pl.BlockSpec(memory_space=pltpu.HBM)
VMEM = pl.BlockSpec(memory_space=pltpu.VMEM)
SDS = jax.ShapeDtypeStruct
PAIR = SDS((2, HD, ENC_D), BF)
SOLO = SDS((1, HD, ENC_D), BF)
ROWS = SDS((SLOTS, NBL, ENC_D), BF)
HEAD_OUT = SDS((2, 4, 128, HD), BF)
GRAD = SDS((SLOTS * NBL, 1024), BF)
TOKENS = SLOTS * NBL


def params(mib):
    return pltpu.CompilerParams(vmem_limit_bytes=mib * 1024 * 1024)


def dot(a, b, dims):
    return lax.dot_general(a, b, (dims, ((), ())), preferred_element_type=F32)


def scratch(shape, dtype=BF):
    return pltpu.VMEM(shape, dtype)


def slot_value(ids, pids, which, s):
    index = which * 4 + lax.rem(s, 4) if not isinstance(s, int) else which * 4 + s % 4
    return jnp.where(s < 4, ids[index], pids[index])


def fetch_rows(pos, ids, pids, sources, rows, sem):
    y, c = pos[1], pos[3]

    def fetch(s, carry):
        owner = slot_value(ids, pids, 0, s)
        row = slot_value(ids, pids, 1, s)
        away = lax.rem(owner // 2 + NY - y, NY)
        other = lax.rem(owner, 2) != c
        for side in range(2):
            here = other if side else jnp.logical_not(other)
            core = 1 - c if side else c
            own, fwd, rev, far = sources[4 * side:4 * side + 4]
            for place, buf in ((0, own), (3 - 2 * core, fwd), (1 + 2 * core, rev), (2, far)):
                @pl.when(jnp.logical_and(here, away == place))
                def _():
                    pltpu.make_async_copy(buf.at[row], rows.at[s], sem.at[s]).start()
        return carry

    lax.fori_loop(0, SLOTS, fetch, 0)


def fetch_weights(pos, own, fwd, rev, far, weight, sem):
    c = pos[3]
    for xx in range(NX):
        away = lax.rem(xx + NX - pos[0], NX)
        place = (xx % 2) * 2 + xx // 2
        for j in range(2):
            for value, src in ((0, own), (3 - 2 * c, fwd), (1 + 2 * c, rev), (2, far)):
                @pl.when(away == value)
                def _():
                    pltpu.make_async_copy(src.at[j], weight.at[j, place], sem.at[j]).start()


def fetch_heads(pos, first, arrays, amat, sem):
    amat[:, :, 0:GROUP, HD:] = jnp.zeros((4, 4, GROUP, HD), BF)
    amat[:, :, GROUP:, 0:HD] = jnp.zeros((4, 4, GROUP, HD), BF)
    for j in range(2):
        col = column_of(pos[2], pos[3], first + j)
        for hi in range(2):
            lanes = pl.ds(pl.multiple_of((hi * NZ + col) * HD, HD), HD)
            for g in range(4):
                there = pl.ds((g % 2) * GROUP, GROUP)
                for kind in range(2):
                    src = arrays[g // 2].at[kind, there, lanes]
                    here = pl.ds(kind * GROUP, GROUP), pl.ds(kind * HD, HD)
                    pltpu.make_async_copy(src, amat.at[2 * j + hi, g, here[0], here[1]], sem).start()


def wait_heads(arrays, amat, sem):
    half = amat.at[:, :, 0:GROUP]
    pltpu.make_async_copy(half, half, sem).wait()


def bundle_math(ids, pids, rows, weight, w_sem, amat, kv, grad, heads):
    scale = HD ** -0.5
    lane = lax.broadcasted_iota(jnp.int32, (GROUP, 2 * NBL), 1)
    live = []
    for g in range(4):
        live0 = NBL - slot_value(ids, pids, 2, 2 * g)
        live1 = NBL - slot_value(ids, pids, 2, 2 * g + 1)
        live.append(lane < jnp.where(lane < NBL, live0, live1 + NBL))
    for j in range(2):
        pltpu.make_async_copy(weight.at[j], weight.at[j], w_sem.at[j]).wait()
        enc = rows[...].reshape(TOKENS, ENC_D)
        kv[j] = dot(enc, weight[j].reshape(512, ENC_D), ((1,), (1,))).astype(BF)

    def begin(j, g, hi):
        both = kv[j, g * 256:(g + 1) * 256, hi * 256:(hi + 1) * 256]
        mat = amat[2 * j + hi, g]
        return both, mat, dot(mat, both, ((1,), (1,)))

    steps = [(j, g, hi) for j in range(2) for g in range(4) for hi in range(2)]
    ahead = begin(*steps[0])
    for n, (j, g, hi) in enumerate(steps):
        both, mat, sd = ahead
        if n + 1 < len(steps):
            ahead = begin(*steps[n + 1])
        s = jnp.where(live[g], sd[:GROUP] * scale, NEG)
        e = jnp.exp(s - jnp.max(s, axis=1, keepdims=True))
        p = e * (1.0 / jnp.sum(e, axis=1, keepdims=True))
        dp = sd[GROUP:]
        delta = jnp.sum(p * dp, axis=1, keepdims=True)
        ds = p * (dp - delta) * scale
        pm = jnp.concatenate([ds.astype(BF), p.astype(BF)], axis=0)
        out = dot(pm, both, ((1,), (0,)))
        spot = pl.ds((g % 2) * GROUP, GROUP)
        heads[g // 2, 0, 2 * j + hi, spot] = out[GROUP:, HD:].astype(BF)
        heads[g // 2, 1, 2 * j + hi, spot] = out[:GROUP, :HD].astype(BF)
        cols = j * 512 + hi * 256
        grad[g * 256:(g + 1) * 256, cols:cols + 256] = dot(pm, mat, ((0,), (0,))).astype(BF)


def back_terms(grad, weight, terms, before=None):
    def back(t, carry):
        here = pl.ds(pl.multiple_of(t * 256, 256), 256)
        total = dot(grad[here], weight[...].reshape(1024, ENC_D), ((1,), (0,)))
        if before is not None:
            total = total + before[pl.ds(2 * t, 2)].reshape(256, ENC_D).astype(F32)
        terms[pl.ds(2 * t, 2)] = total.astype(BF).reshape(2, NBL, ENC_D)
        return carry

    lax.fori_loop(0, 4, back, 0)


def weight_products(pos, grad, rows, parts):
    for j in range(2):
        for hi in range(2):
            cols = j * 512 + hi * 256
            product = dot(
                grad[:, cols:cols + 256], rows[...].reshape(TOKENS, ENC_D), ((0,), (0,))
            ).astype(BF)
            for kind in range(2):
                away = lax.rem(2 * kind + hi + NX - pos[0], NX)
                parts[away, j] = product[kind * HD:(kind + 1) * HD]


def part_copies(pos, parts, outs, sem):
    own, fwd, rev, far = outs
    c = pos[3]
    pairs = (
        (parts.at[2], far),
        (parts.at[3 - 2 * c], rev),
        (parts.at[1 + 2 * c], fwd),
        (parts.at[0], own),
    )
    return [pltpu.make_async_copy(src, dst, sem.at[n]) for n, (src, dst) in enumerate(pairs)]


PART_OUTS = (PAIR,) * 4


def bundle_kernel(
    base, pos, ids, pids, row_sources, before_in, weights, arrays, terms_out, own_out, par_out, part_outs, rows_out,
    rows, weight, amat, kv, grad, heads, terms, parts, row_sem, w_sem, q_sem, sem, part_sem, before,
):
    copies = []
    if base:
        fetch_rows(pos, ids, pids, row_sources, rows, row_sem)
    else:
        for s in range(SLOTS):
            pltpu.make_async_copy(row_sources[0].at[s], rows.at[s], row_sem.at[s]).start()
        before_copy = pltpu.make_async_copy(before_in, before, sem.at[4])
        before_copy.start()
    fetch_weights(pos, *weights, weight, w_sem)
    fetch_heads(pos, base, arrays, amat, q_sem)
    for s in range(SLOTS):
        pltpu.make_async_copy(rows.at[s], rows.at[s], row_sem.at[s]).wait()
    if base:
        copies.append(pltpu.make_async_copy(rows, rows_out, sem.at[0]))
        copies[-1].start()
    wait_heads(arrays, amat, q_sem)
    bundle_math(ids, pids, rows, weight, w_sem, amat, kv, grad, heads)
    for n, out in enumerate((own_out, par_out)):
        copies.append(pltpu.make_async_copy(heads.at[n], out, sem.at[1 + n]))
        copies[-1].start()
    if base:
        weight_products(pos, grad, rows, parts)
        outs = part_copies(pos, parts, part_outs, part_sem)
        back_terms(grad, weight, terms)
    else:
        outs = [pltpu.make_async_copy(grad, part_outs[0], part_sem.at[0])]
        before_copy.wait()
        back_terms(grad, weight, terms, before)
    outs.append(pltpu.make_async_copy(terms, terms_out, sem.at[3]))
    for copy in outs:
        copy.start()
    for copy in copies + outs:
        copy.wait()


def first_kernel(pos, ids, pids, *refs):
    sources, weights, arrays, refs = refs[:8], refs[8:12], refs[12:14], refs[14:]
    rows_out, terms_out, own_out, par_out, refs = *refs[:4], refs[4:]
    part_outs, refs = refs[:4], refs[4:]
    bundle_kernel(
        2, pos, ids, pids, sources, None, weights, arrays, terms_out, own_out, par_out, part_outs, rows_out, *refs, None
    )


def second_kernel(pos, ids, pids, *refs):
    sources, before_in, weights, arrays, refs = refs[:1], refs[1], refs[2:6], refs[6:8], refs[8:]
    terms_out, own_out, par_out, refs = *refs[:3], refs[3:]
    part_outs, refs = refs[:1], refs[1:]
    bundle_kernel(
        0, pos, ids, pids, sources, before_in, weights, arrays, terms_out, own_out, par_out, part_outs, None, *refs
    )


def bundle(kernel, name, out_shape, extra, pos, ids, pids, *arrays):
    return pl.pallas_call(
        kernel,
        out_shape=out_shape,
        grid_spec=pltpu.PrefetchScalarGridSpec(
            num_scalar_prefetch=3,
            grid=(),
            in_specs=[HBM] * len(arrays),
            out_specs=[HBM] * len(out_shape),
            scratch_shapes=[
                scratch((SLOTS, NBL, ENC_D)),
                scratch((2, 4, HD, ENC_D)),
                scratch((4, 4, 128, 256)),
                scratch((2, TOKENS, 512)),
                scratch((TOKENS, 1024)),
                scratch((2, 2, 4, 128, HD)),
                scratch((SLOTS, NBL, ENC_D)),
                scratch((4, 2, HD, ENC_D)),
                pltpu.SemaphoreType.DMA((SLOTS,)),
                pltpu.SemaphoreType.DMA((2,)),
                pltpu.SemaphoreType.DMA,
                pltpu.SemaphoreType.DMA((5,)),
                pltpu.SemaphoreType.DMA((4,)),
            ] + extra,
        ),
        compiler_params=params(60),
        cost_estimate=pl.CostEstimate(flops=6_000_000_000, bytes_accessed=16_000_000, transcendentals=300_000),
        name=name,
    )(pos, ids, pids, *arrays)


def first(*args):
    return bundle(first_kernel, "first_heads", (ROWS, ROWS, HEAD_OUT, HEAD_OUT) + PART_OUTS, [], *args)


def second(*args):
    return bundle(
        second_kernel, "second_heads", (ROWS, HEAD_OUT, HEAD_OUT, GRAD), [scratch((SLOTS, NBL, ENC_D))], *args
    )


def weight_kernel(pos, grad_in, rows_in, *refs):
    part_outs, refs = refs[:4], refs[4:]
    grad, rows, parts, sem, part_sem = refs
    loads = [
        pltpu.make_async_copy(rows_in, rows, sem.at[0]),
        pltpu.make_async_copy(grad_in, grad, sem.at[1]),
    ]
    for copy in loads:
        copy.start()
    for copy in loads:
        copy.wait()
    weight_products(pos, grad, rows, parts)
    outs = part_copies(pos, parts, part_outs, part_sem)
    for copy in outs:
        copy.start()
    for copy in outs:
        copy.wait()


def weight_parts(pos, grad, rows):
    return pl.pallas_call(
        weight_kernel,
        out_shape=PART_OUTS,
        grid_spec=pltpu.PrefetchScalarGridSpec(
            num_scalar_prefetch=1,
            grid=(),
            in_specs=[HBM] * 2,
            out_specs=[HBM] * 4,
            scratch_shapes=[
                scratch((TOKENS, 1024)),
                scratch((SLOTS, NBL, ENC_D)),
                scratch((4, 2, HD, ENC_D)),
                pltpu.SemaphoreType.DMA((2,)),
                pltpu.SemaphoreType.DMA((4,)),
            ],
        ),
        compiler_params=params(40),
        cost_estimate=pl.CostEstimate(flops=1_900_000_000, bytes_accessed=6_000_000, transcendentals=0),
        name="weight_parts",
    )(pos, grad, rows)


def near_kernel(pos, *refs):
    values, outs = refs[:4], refs[4:]
    c = pos[3]
    for j in range(2):
        total = values[0][j].astype(F32)
        for value in values[1:]:
            total = total + value[j].astype(F32)
        total = total.astype(BF)
        low, high = total[:64], total[64:]
        outs[j][...] = jnp.where(c == 0, low, high)
        outs[2 + j][...] = jnp.where(c == 0, high, low)


def near_halves(pos, *values):
    return pl.pallas_call(
        near_kernel,
        out_shape=(SDS((64, ENC_D), BF),) * 4,
        grid_spec=pltpu.PrefetchScalarGridSpec(
            num_scalar_prefetch=1, grid=(), in_specs=[VMEM] * 4, out_specs=[VMEM] * 4
        ),
        compiler_params=params(16),
        cost_estimate=pl.CostEstimate(flops=1_000_000, bytes_accessed=2_500_000, transcendentals=0),
        name="near_halves",
    )(pos, *values)


def route_kernel(pos, ids, pids, terms, p_terms, own, fwd, rev, far, total):
    y, c = pos[1], pos[3]
    total[...] = jnp.zeros_like(total)
    for s in range(SLOTS):
        src = ids if s < 4 else pids
        owner, row = src[s % 4], src[4 + s % 4]

        @pl.when(lax.rem(owner, 2) == c)
        def _():
            place = lax.rem(owner // 2 + NY - y, NY) * 4 + row
            total[place] = total[place] + (terms[s].astype(F32) + p_terms[s ^ 4].astype(F32))

    far[...] = total[8:12].astype(BF)
    rev[...] = total[pl.ds(12 - 8 * c, 4)].astype(BF)
    fwd[...] = total[pl.ds(4 + 8 * c, 4)].astype(BF)
    own[...] = total[0:4].astype(BF)


def route(pos, ids, pids, terms, p_terms):
    return pl.pallas_call(
        route_kernel,
        out_shape=(SDS((4, NBL, ENC_D), BF),) * 4,
        grid_spec=pltpu.PrefetchScalarGridSpec(
            num_scalar_prefetch=3,
            grid=(),
            in_specs=[VMEM] * 2,
            out_specs=[VMEM] * 4,
            scratch_shapes=[scratch((16, NBL, ENC_D), F32)],
        ),
        compiler_params=params(40),
        cost_estimate=pl.CostEstimate(flops=10_000_000, bytes_accessed=8_000_000, transcendentals=0),
        name="route",
    )(pos, ids, pids, terms, p_terms)


def join_kernel(pos, own_a, own_b, got_a, got_b, att_out, dq_out):
    z, c = pos[2], pos[3]
    for j in range(4):
        for core, (a, b) in ((c, (own_a, own_b)), (1 - c, (got_a, got_b))):
            src = b if j < 2 else a
            col = column_of(z, core, j)
            for hi in range(2):
                lanes = pl.ds(pl.multiple_of((hi * NZ + col) * HD, HD), HD)
                att_out[:, lanes] = src[0, 2 * (j % 2) + hi]
                dq_out[:, lanes] = src[1, 2 * (j % 2) + hi]


def join(pos, *arrays):
    return pl.pallas_call(
        join_kernel,
        out_shape=(SDS((128, HQ), BF),) * 2,
        grid_spec=pltpu.PrefetchScalarGridSpec(
            num_scalar_prefetch=1, grid=(), in_specs=[VMEM] * 4, out_specs=[VMEM] * 2
        ),
        compiler_params=params(16),
        cost_estimate=pl.CostEstimate(flops=0, bytes_accessed=4_000_000, transcendentals=0),
        name="join",
    )(pos, *arrays)


def add(*values):
    total = values[0].astype(F32)
    for value in values[1:]:
        total = total + value.astype(F32)
    return total


def tie(*values):
    return lax.optimization_barrier(values)


def on_device(queries, encodings, weight, shard, row, pad, cotangent):
    dp, ctx = lax.axis_index("dp"), lax.axis_index("ctx")
    pos = jnp.stack([dp // NZ, ctx // 2, dp % NZ, ctx % 2]).astype(jnp.int32)
    core = ctx % 2
    ids = jnp.concatenate([shard.reshape(4), row.reshape(4), pad.reshape(4)])
    q = queries.reshape(128, HQ)
    cot = cotangent.reshape(128, HQ)
    enc = encodings.reshape(4, NBL, ENC_D)

    y1, u1, u0, pids = send(enc, Y_FWD), send(weight, Z_OUT[1]), send(weight, Z_OUT[0]), send(ids, SWAP)
    p_own = send(enc, SWAP)
    ub = jnp.stack([u0, u1])
    heads_in = jnp.stack([q, cot])
    y1, ub, pids, p_own, enc_2, heads_2 = tie(y1, ub, pids, p_own, enc, heads_in)
    y2, ua, b1, b2 = send(enc_2, Y_REV), send(ub, Z_PAIR_OUT), send(ub, X_FWD), send(ub, X_REV)
    p_y1 = send(y1, SWAP)
    y1, y2, ua, b1, p_y1, b2, heads_2 = tie(y1, y2, ua, b1, p_y1, b2, heads_2)
    y3, a1, a2 = send(y1, Y_FWD), send(ua, X_FWD), send(ua, X_REV)
    heads_par, p_y2 = send(heads_2, SWAP), send(y2, SWAP)
    y3, a1, a2, heads_par, p_y2 = tie(y3, a1, a2, heads_par, p_y2)
    a3, p_y3 = send(a1, X_FWD), send(y3, SWAP)
    a3, p_y3, b1 = tie(a3, p_y3, b1)
    b3 = send(b1, X_FWD)

    rows, terms_a, own_a, par_a, *parts_a = first(
        pos, ids, pids, enc, y1, y2, y3, p_own, p_y1, p_y2, p_y3, ua, a1, a2, a3, heads_in, heads_par
    )
    got_a = send(par_a, SWAP)
    ga_own, ga_fwd, ga_rev, ga_far = parts_a
    ga1, ga2 = send(ga_far, X_FWD), send(ga_rev, X_REV)
    terms, own_b, par_b, grad = second(
        pos, ids, pids, rows, terms_a, ub, b1, b2, b3, heads_in, heads_par
    )
    terms, ga1, ga2, got_a = tie(terms, ga1, ga2, got_a)
    p_terms = send(terms, SWAP)
    ga3 = send(add(ga_fwd, ga1).astype(BF), X_FWD)
    gb_own, gb_fwd, gb_rev, gb_far = weight_parts(pos, grad, rows)
    gb1, gb2 = send(gb_far, X_FWD), send(gb_rev, X_REV)
    far = send(add(ga_own, ga2, ga3).astype(BF), Z_PAIR_BACK)
    e_own, e_fwd, e_rev, e_far = route(pos, ids, pids, terms, p_terms)
    e1 = send(e_far, Y_FWD)
    gb1, gb2, _ = tie(gb1, gb2, e_far)
    gb3 = send(add(gb_fwd, gb1).astype(BF), X_FWD)
    e_rev, gb2, far = tie(e_rev, gb2, far)
    e2 = send(e_rev, Y_REV)
    e1, gb3 = tie(e1, gb3)
    s0, s1, t0, t1 = near_halves(pos, gb_own, gb2, gb3, far)
    s0, s1 = send(s0, Z_BACK[0]), send(s1, Z_BACK[1])
    t0, t1 = send(t0, Z_BACK_ACROSS[0]), send(t1, Z_BACK_ACROSS[1])
    e3_in = add(e_fwd, e1).astype(BF)
    e3_in, e2, s0, s1, t0, t1, par_b = tie(e3_in, e2, s0, s1, t0, t1, par_b)
    half = add(s0, s1, t0, t1).astype(BF)
    e3 = send(e3_in, Y_FWD)
    got_b = send(par_b, SWAP)
    half = add(half, send(half, Y_UP), send(half, Y_DN), send(half, Y_TWO))
    half, e3, got_b = tie(half, e3, got_b)
    rest = send(half, SWAP)
    low = jnp.where(core == 0, half, rest)
    high = jnp.where(core == 0, rest, half)
    weight_gradient = jnp.concatenate([low, high])

    enc_grad = add(e_own, e2, e3).astype(BF)
    att, dq = join(pos, own_a, own_b, got_a, got_b)
    return (
        att.reshape(1, 128, HQ),
        dq.reshape(1, 128, HQ),
        enc_grad.reshape(1, 4, NBL, ENC_D),
        weight_gradient,
    )


def solution(mesh):
    rows = P("dp", "ctx", None)
    return jax.shard_map(
        on_device,
        mesh=mesh,
        in_specs=(rows, P("dp", "ctx", None, None), P("dp", None), rows, rows, rows, rows),
        out_specs=(rows, rows, P("dp", "ctx", None, None), P("dp", None)),
        check_vma=False,
    )
```

```python
import functools

import jax
import jax.numpy as jnp
from jax import lax
from jax.experimental import pallas as pl
from jax.experimental.pallas import tpu as pltpu
from jax.sharding import PartitionSpec as P

HEADS = 16
HD = 128
ENC_D = 896
NBL = 128
GROUP = 64
HQ = 2048
NX, NY, NZ = 4, 4, 8
SLOTS = 8
NEG = -1e30
BF = jnp.bfloat16
F32 = jnp.float32
AXES = ("dp", "ctx")


def _lin(x, y, z, c):
    return ((x % NX) * NZ + z % NZ) * (NY * 2) + (y % NY) * 2 + c


def _pairs(move):
    return [
        (_lin(x, y, z, c), _lin(*move(x, y, z, c)))
        for x in range(NX)
        for z in range(NZ)
        for y in range(NY)
        for c in range(2)
    ]


Y_UP = _pairs(lambda x, y, z, c: (x, y + 1, z, c))
Y_DN = _pairs(lambda x, y, z, c: (x, y - 1, z, c))
Y_TWO = _pairs(lambda x, y, z, c: (x, y + 2, z, c))
Y_FWD = _pairs(lambda x, y, z, c: (x, y + 1 - 2 * c, z, c))
Y_REV = _pairs(lambda x, y, z, c: (x, y - 1 + 2 * c, z, c))
X_FWD = _pairs(lambda x, y, z, c: (x + 1 - 2 * c, y, z, c))
X_REV = _pairs(lambda x, y, z, c: (x - 1 + 2 * c, y, z, c))
X_TWO = _pairs(lambda x, y, z, c: (x + 2, y, z, c))
SWAP = _pairs(lambda x, y, z, c: (x, y, z, 1 - c))
Z_OUT = [_pairs(lambda x, y, z, c, j=j: (x, y, z + j if c == 0 else z - 1 - j, c)) for j in range(4)]
Z_BACK = [_pairs(lambda x, y, z, c, j=j: (x, y, z - j if c == 0 else z + 1 + j, c)) for j in range(2)]
Z_BACK_ACROSS = [
    _pairs(lambda x, y, z, c, j=j: (x, y, z - j if c == 0 else z + 1 + j, 1 - c)) for j in range(2)
]
Z_PAIR_BACK = _pairs(lambda x, y, z, c: (x, y, z - 2 + 4 * c, c))


def send(value, pairs):
    return lax.ppermute(value, AXES, pairs)


def column_of(z, c, j):
    return lax.rem(jnp.where(c == 0, z + NZ - j, z + 1 + j), NZ)


HBM = pl.BlockSpec(memory_space=pltpu.HBM)
VMEM = pl.BlockSpec(memory_space=pltpu.VMEM)
SDS = jax.ShapeDtypeStruct
PAIR = SDS((2, HD, ENC_D), BF)
SOLO = SDS((1, HD, ENC_D), BF)
ROWS = SDS((SLOTS, NBL, ENC_D), BF)
HEAD_OUT = SDS((2, 4, 128, HD), BF)
TOKENS = SLOTS * NBL


def params(mib):
    return pltpu.CompilerParams(vmem_limit_bytes=mib * 1024 * 1024)


def dot(a, b, dims):
    return lax.dot_general(a, b, (dims, ((), ())), preferred_element_type=F32)


def scratch(shape, dtype=BF):
    return pltpu.VMEM(shape, dtype)


def slot_value(ids, pids, which, s):
    index = which * 4 + lax.rem(s, 4) if not isinstance(s, int) else which * 4 + s % 4
    return jnp.where(s < 4, ids[index], pids[index])


def fetch_rows(pos, ids, pids, sources, rows, sem):
    y, c = pos[1], pos[3]

    def fetch(s, carry):
        owner = slot_value(ids, pids, 0, s)
        row = slot_value(ids, pids, 1, s)
        away = lax.rem(owner // 2 + NY - y, NY)
        other = lax.rem(owner, 2) != c
        for side in range(2):
            here = other if side else jnp.logical_not(other)
            core = 1 - c if side else c
            own, fwd, rev, far = sources[4 * side:4 * side + 4]
            for place, buf in ((0, own), (3 - 2 * core, fwd), (1 + 2 * core, rev), (2, far)):
                @pl.when(jnp.logical_and(here, away == place))
                def _():
                    pltpu.make_async_copy(buf.at[row], rows.at[s], sem.at[s]).start()
        return carry

    lax.fori_loop(0, SLOTS, fetch, 0)


def fetch_weights(pos, own, fwd, rev, far, weight, sem):
    c = pos[3]
    for xx in range(NX):
        away = lax.rem(xx + NX - pos[0], NX)
        place = (xx % 2) * 2 + xx // 2
        for j in range(2):
            for value, src in ((0, own), (3 - 2 * c, fwd), (1 + 2 * c, rev), (2, far)):
                @pl.when(away == value)
                def _():
                    pltpu.make_async_copy(src.at[j], weight.at[j, place], sem.at[j]).start()


def fetch_heads(pos, first, arrays, amat, sem):
    amat[:, :, 0:GROUP, HD:] = jnp.zeros((4, 4, GROUP, HD), BF)
    amat[:, :, GROUP:, 0:HD] = jnp.zeros((4, 4, GROUP, HD), BF)
    for j in range(2):
        col = column_of(pos[2], pos[3], first + j)
        for hi in range(2):
            lanes = pl.ds(pl.multiple_of((hi * NZ + col) * HD, HD), HD)
            for g in range(4):
                there = pl.ds((g % 2) * GROUP, GROUP)
                for kind in range(2):
                    src = arrays[g // 2].at[kind, there, lanes]
                    here = pl.ds(kind * GROUP, GROUP), pl.ds(kind * HD, HD)
                    pltpu.make_async_copy(src, amat.at[2 * j + hi, g, here[0], here[1]], sem).start()


def wait_heads(amat, sem):
    half = amat.at[:, :, 0:GROUP]
    pltpu.make_async_copy(half, half, sem).wait()


def bundle_math(ids, pids, rows, weight, w_sem, amat, kv, grad, heads, q_sem):
    scale = HD ** -0.5
    lane = lax.broadcasted_iota(jnp.int32, (GROUP, 2 * NBL), 1)
    live = []
    for g in range(4):
        live0 = NBL - slot_value(ids, pids, 2, 2 * g)
        live1 = NBL - slot_value(ids, pids, 2, 2 * g + 1)
        live.append(lane < jnp.where(lane < NBL, live0, live1 + NBL))
    for j in range(2):
        pltpu.make_async_copy(weight.at[j], weight.at[j], w_sem.at[j]).wait()
        enc = rows[...].reshape(TOKENS, ENC_D)
        kv[j] = dot(enc, weight[j].reshape(512, ENC_D), ((1,), (1,))).astype(BF)
    wait_heads(amat, q_sem)

    def begin(j, g, hi):
        both = kv[j, g * 256:(g + 1) * 256, hi * 256:(hi + 1) * 256]
        mat = amat[2 * j + hi, g]
        return both, mat, dot(mat, both, ((1,), (1,)))

    steps = [(j, g, hi) for j in range(2) for g in range(4) for hi in range(2)]
    ahead = begin(*steps[0])
    for n, (j, g, hi) in enumerate(steps):
        both, mat, sd = ahead
        if n + 1 < len(steps):
            ahead = begin(*steps[n + 1])
        s = jnp.where(live[g], sd[:GROUP] * scale, NEG)
        e = jnp.exp(s - jnp.max(s, axis=1, keepdims=True))
        p = e * (1.0 / jnp.sum(e, axis=1, keepdims=True))
        dp = sd[GROUP:]
        delta = jnp.sum(p * dp, axis=1, keepdims=True)
        ds = p * (dp - delta) * scale
        pm = jnp.concatenate([ds.astype(BF), p.astype(BF)], axis=0)
        out = dot(pm, both, ((1,), (0,)))
        spot = pl.ds((g % 2) * GROUP, GROUP)
        heads[g // 2, 0, 2 * j + hi, spot] = out[GROUP:, HD:].astype(BF)
        heads[g // 2, 1, 2 * j + hi, spot] = out[:GROUP, :HD].astype(BF)
        cols = j * 512 + hi * 256
        grad[g * 256:(g + 1) * 256, cols:cols + 256] = dot(pm, mat, ((0,), (0,))).astype(BF)


def back_terms(grad, weight, terms, before=None):
    def back(t, carry):
        here = pl.ds(pl.multiple_of(t * 256, 256), 256)
        total = dot(grad[here], weight[...].reshape(1024, ENC_D), ((1,), (0,)))
        if before is not None:
            total = total + before[pl.ds(2 * t, 2)].reshape(256, ENC_D).astype(F32)
        terms[pl.ds(2 * t, 2)] = total.astype(BF).reshape(2, NBL, ENC_D)
        return carry

    lax.fori_loop(0, 4, back, 0)


def weight_products(pos, grad, rows, parts):
    for j in range(2):
        for hi in range(2):
            cols = j * 512 + hi * 256
            product = dot(
                grad[:, cols:cols + 256], rows[...].reshape(TOKENS, ENC_D), ((0,), (0,))
            ).astype(BF)
            for kind in range(2):
                away = lax.rem(2 * kind + hi + NX - pos[0], NX)
                parts[away, j] = product[kind * HD:(kind + 1) * HD]


def part_copies(pos, parts, outs, sem):
    own, fwd, rev, far = outs
    c = pos[3]
    pairs = (
        (parts.at[2], far),
        (parts.at[3 - 2 * c], rev),
        (parts.at[1 + 2 * c], fwd),
        (parts.at[0], own),
    )
    return [pltpu.make_async_copy(src, dst, sem.at[n]) for n, (src, dst) in enumerate(pairs)]


PART_OUTS = (PAIR,) * 4


def bundle_kernel(
    base, pos, ids, pids, row_sources, before_in, weights, arrays, terms_out, own_out, par_out, part_outs, rows_out,
    rows, weight, amat, kv, grad, heads, terms, parts, row_sem, w_sem, q_sem, sem, part_sem, before,
):
    copies = []
    if base:
        fetch_rows(pos, ids, pids, row_sources, rows, row_sem)
    else:
        for s in range(SLOTS):
            pltpu.make_async_copy(row_sources[0].at[s], rows.at[s], row_sem.at[s]).start()
        before_copy = pltpu.make_async_copy(before_in, before, sem.at[4])
        before_copy.start()
    fetch_weights(pos, *weights, weight, w_sem)
    fetch_heads(pos, base, arrays, amat, q_sem)
    for s in range(SLOTS):
        pltpu.make_async_copy(rows.at[s], rows.at[s], row_sem.at[s]).wait()
    if base:
        copies.append(pltpu.make_async_copy(rows, rows_out, sem.at[0]))
        copies[-1].start()
    bundle_math(ids, pids, rows, weight, w_sem, amat, kv, grad, heads, q_sem)
    for n, out in enumerate((own_out, par_out)):
        copies.append(pltpu.make_async_copy(heads.at[n], out, sem.at[1 + n]))
        copies[-1].start()
    if base:
        weight_products(pos, grad, rows, parts)
        outs = part_copies(pos, parts, part_outs, part_sem)
        for copy in outs:
            copy.start()
        back_terms(grad, weight, terms)
    else:
        before_copy.wait()
        back_terms(grad, weight, terms, before)
    copies.append(pltpu.make_async_copy(terms, terms_out, sem.at[3]))
    copies[-1].start()
    if not base:
        weight_products(pos, grad, rows, parts)
        outs = part_copies(pos, parts, part_outs, part_sem)
        for copy in outs:
            copy.start()
    for copy in copies + outs:
        copy.wait()


def first_kernel(pos, ids, pids, *refs):
    sources, weights, arrays, refs = refs[:8], refs[8:12], refs[12:14], refs[14:]
    rows_out, terms_out, own_out, par_out, refs = *refs[:4], refs[4:]
    part_outs, refs = refs[:4], refs[4:]
    bundle_kernel(
        2, pos, ids, pids, sources, None, weights, arrays, terms_out, own_out, par_out, part_outs, rows_out, *refs, None
    )


def second_kernel(pos, ids, pids, *refs):
    sources, before_in, weights, arrays, refs = refs[:1], refs[1], refs[2:6], refs[6:8], refs[8:]
    terms_out, own_out, par_out, refs = *refs[:3], refs[3:]
    part_outs, refs = refs[:4], refs[4:]
    bundle_kernel(
        0, pos, ids, pids, sources, before_in, weights, arrays, terms_out, own_out, par_out, part_outs, None, *refs
    )


def bundle(kernel, name, out_shape, extra, pos, ids, pids, *arrays):
    return pl.pallas_call(
        kernel,
        out_shape=out_shape,
        grid_spec=pltpu.PrefetchScalarGridSpec(
            num_scalar_prefetch=3,
            grid=(),
            in_specs=[HBM] * len(arrays),
            out_specs=[HBM] * len(out_shape),
            scratch_shapes=[
                scratch((SLOTS, NBL, ENC_D)),
                scratch((2, 4, HD, ENC_D)),
                scratch((4, 4, 128, 256)),
                scratch((2, TOKENS, 512)),
                scratch((TOKENS, 1024)),
                scratch((2, 2, 4, 128, HD)),
                scratch((SLOTS, NBL, ENC_D)),
                scratch((4, 2, HD, ENC_D)),
                pltpu.SemaphoreType.DMA((SLOTS,)),
                pltpu.SemaphoreType.DMA((2,)),
                pltpu.SemaphoreType.DMA,
                pltpu.SemaphoreType.DMA((5,)),
                pltpu.SemaphoreType.DMA((4,)),
            ] + extra,
        ),
        compiler_params=params(60),
        cost_estimate=pl.CostEstimate(flops=6_000_000_000, bytes_accessed=16_000_000, transcendentals=300_000),
        name=name,
    )(pos, ids, pids, *arrays)


def first(*args):
    return bundle(first_kernel, "first_heads", (ROWS, ROWS, HEAD_OUT, HEAD_OUT) + PART_OUTS, [], *args)


def second(*args):
    return bundle(
        second_kernel, "second_heads", (ROWS, HEAD_OUT, HEAD_OUT) + PART_OUTS, [scratch((SLOTS, NBL, ENC_D))], *args
    )


def near_kernel(pos, *refs):
    values, outs = refs[:4], refs[4:]
    c = pos[3]
    for j in range(2):
        total = values[0][j].astype(F32)
        for value in values[1:]:
            total = total + value[j].astype(F32)
        total = total.astype(BF)
        low, high = total[:64], total[64:]
        outs[j][...] = jnp.where(c == 0, low, high)
        outs[2 + j][...] = jnp.where(c == 0, high, low)


def near_halves(pos, *values):
    return pl.pallas_call(
        near_kernel,
        out_shape=(SDS((64, ENC_D), BF),) * 4,
        grid_spec=pltpu.PrefetchScalarGridSpec(
            num_scalar_prefetch=1, grid=(), in_specs=[VMEM] * 4, out_specs=[VMEM] * 4
        ),
        compiler_params=params(16),
        cost_estimate=pl.CostEstimate(flops=1_000_000, bytes_accessed=2_500_000, transcendentals=0),
        name="near_halves",
    )(pos, *values)


def route_kernel(pos, ids, pids, terms, p_terms, own, fwd, rev, far, total):
    y, c = pos[1], pos[3]
    total[...] = jnp.zeros_like(total)
    for s in range(SLOTS):
        src = ids if s < 4 else pids
        owner, row = src[s % 4], src[4 + s % 4]

        @pl.when(lax.rem(owner, 2) == c)
        def _():
            place = lax.rem(owner // 2 + NY - y, NY) * 4 + row
            total[place] = total[place] + (terms[s].astype(F32) + p_terms[s ^ 4].astype(F32))

    far[...] = total[8:12].astype(BF)
    rev[...] = total[pl.ds(12 - 8 * c, 4)].astype(BF)
    fwd[...] = total[pl.ds(4 + 8 * c, 4)].astype(BF)
    own[...] = total[0:4].astype(BF)


def route(pos, ids, pids, terms, p_terms):
    return pl.pallas_call(
        route_kernel,
        out_shape=(SDS((4, NBL, ENC_D), BF),) * 4,
        grid_spec=pltpu.PrefetchScalarGridSpec(
            num_scalar_prefetch=3,
            grid=(),
            in_specs=[VMEM] * 2,
            out_specs=[VMEM] * 4,
            scratch_shapes=[scratch((16, NBL, ENC_D), F32)],
        ),
        compiler_params=params(40),
        cost_estimate=pl.CostEstimate(flops=10_000_000, bytes_accessed=8_000_000, transcendentals=0),
        name="route",
    )(pos, ids, pids, terms, p_terms)


def join_kernel(pos, own_a, own_b, got_a, got_b, att_out, dq_out):
    z, c = pos[2], pos[3]
    for j in range(4):
        for core, (a, b) in ((c, (own_a, own_b)), (1 - c, (got_a, got_b))):
            src = b if j < 2 else a
            col = column_of(z, core, j)
            for hi in range(2):
                lanes = pl.ds(pl.multiple_of((hi * NZ + col) * HD, HD), HD)
                att_out[:, lanes] = src[0, 2 * (j % 2) + hi]
                dq_out[:, lanes] = src[1, 2 * (j % 2) + hi]


def join(pos, *arrays):
    return pl.pallas_call(
        join_kernel,
        out_shape=(SDS((128, HQ), BF),) * 2,
        grid_spec=pltpu.PrefetchScalarGridSpec(
            num_scalar_prefetch=1, grid=(), in_specs=[VMEM] * 4, out_specs=[VMEM] * 2
        ),
        compiler_params=params(16),
        cost_estimate=pl.CostEstimate(flops=0, bytes_accessed=4_000_000, transcendentals=0),
        name="join",
    )(pos, *arrays)


def add(*values):
    total = values[0].astype(F32)
    for value in values[1:]:
        total = total + value.astype(F32)
    return total


def tie(*values):
    return lax.optimization_barrier(values)


def on_device(queries, encodings, weight, shard, row, pad, cotangent):
    dp, ctx = lax.axis_index("dp"), lax.axis_index("ctx")
    pos = jnp.stack([dp // NZ, ctx // 2, dp % NZ, ctx % 2]).astype(jnp.int32)
    core = ctx % 2
    ids = jnp.concatenate([shard.reshape(4), row.reshape(4), pad.reshape(4)])
    q = queries.reshape(128, HQ)
    cot = cotangent.reshape(128, HQ)
    enc = encodings.reshape(4, NBL, ENC_D)

    y1, y2, p_own, pids = send(enc, Y_FWD), send(enc, Y_REV), send(enc, SWAP), send(ids, SWAP)
    u3, u2 = send(weight, Z_OUT[3]), send(weight, Z_OUT[2])
    ua = jnp.stack([u2, u3])
    ua, y1, y2, p_own, pids, weight_2 = tie(ua, y1, y2, p_own, pids, weight)
    a1, a2, y3 = send(ua, X_FWD), send(ua, X_REV), send(y1, Y_FWD)
    u1, u0 = send(weight_2, Z_OUT[1]), send(weight_2, Z_OUT[0])
    ub = jnp.stack([u0, u1])
    heads_in = jnp.stack([q, cot])
    a1, a2, y3, ub, y1, y2, heads_in = tie(a1, a2, y3, ub, y1, y2, heads_in)
    a3, heads_par = send(a1, X_FWD), send(heads_in, SWAP)
    p_y1, p_y2, p_y3 = send(y1, SWAP), send(y2, SWAP), send(y3, SWAP)
    a3, p_y1, p_y2, p_y3, heads_par, ub = tie(a3, p_y1, p_y2, p_y3, heads_par, ub)
    b1, b2, b3 = send(ub, X_FWD), send(ub, X_REV), send(ub, X_TWO)

    rows, terms_a, own_a, par_a, *parts_a = first(
        pos, ids, pids, enc, y1, y2, y3, p_own, p_y1, p_y2, p_y3, ua, a1, a2, a3, heads_in, heads_par
    )
    got_a = send(par_a, SWAP)
    ga_own, ga_fwd, ga_rev, ga_far = parts_a
    ga1, ga2 = send(ga_far, X_FWD), send(ga_rev, X_REV)
    terms, own_b, par_b, gb_own, gb_fwd, gb_rev, gb_far = second(
        pos, ids, pids, rows, terms_a, ub, b1, b2, b3, heads_in, heads_par
    )
    terms, ga1, ga2, got_a = tie(terms, ga1, ga2, got_a)
    p_terms = send(terms, SWAP)
    ga3 = send(add(ga_fwd, ga1).astype(BF), X_FWD)
    gb1 = send(gb_far, X_FWD)
    e_own, e_fwd, e_rev, e_far = route(pos, ids, pids, terms, p_terms)
    e1 = send(e_far, Y_FWD)
    ga3, gb1, gb_rev, _ = tie(ga3, gb1, gb_rev, e_far)
    far = send(add(ga_own, ga2, ga3).astype(BF), Z_PAIR_BACK)
    gb3 = send(add(gb_fwd, gb1).astype(BF), X_FWD)
    gb2 = send(gb_rev, X_REV)
    e2 = send(e_rev, Y_REV)
    gb2, gb3, far, e1, e2 = tie(gb2, gb3, far, e1, e2)
    e3 = send(add(e_fwd, e1).astype(BF), Y_FWD)
    s0, s1, t0, t1 = near_halves(pos, gb_own, gb2, gb3, far)
    s0, s1 = send(s0, Z_BACK[0]), send(s1, Z_BACK[1])
    t0, t1 = send(t0, Z_BACK_ACROSS[0]), send(t1, Z_BACK_ACROSS[1])
    s0, s1, t0, t1, par_b, e3 = tie(s0, s1, t0, t1, par_b, e3)
    half = add(s0, s1, t0, t1).astype(BF)
    got_b = send(par_b, SWAP)
    half = add(half, send(half, Y_UP), send(half, Y_DN), send(half, Y_TWO))
    rest = send(half, SWAP)
    low = jnp.where(core == 0, half, rest)
    high = jnp.where(core == 0, rest, half)
    weight_gradient = jnp.concatenate([low, high])

    enc_grad = add(e_own, e2, e3).astype(BF)
    att, dq = join(pos, own_a, own_b, got_a, got_b)
    return (
        att.reshape(1, 128, HQ),
        dq.reshape(1, 128, HQ),
        enc_grad.reshape(1, 4, NBL, ENC_D),
        weight_gradient,
    )


def solution(mesh):
    rows = P("dp", "ctx", None)
    return jax.shard_map(
        on_device,
        mesh=mesh,
        in_specs=(rows, P("dp", "ctx", None, None), P("dp", None), rows, rows, rows, rows),
        out_specs=(rows, rows, P("dp", "ctx", None, None), P("dp", None)),
        check_vma=False,
    )
```

```python
import functools

import jax
import jax.numpy as jnp
from jax import lax
from jax.experimental import pallas as pl
from jax.experimental.pallas import tpu as pltpu
from jax.sharding import PartitionSpec as P

HEADS = 16
HD = 128
ENC_D = 896
NBL = 128
GROUP = 64
HQ = 2048
NX, NY, NZ = 4, 4, 8
SLOTS = 8
NEG = -1e30
BF = jnp.bfloat16
F32 = jnp.float32
AXES = ("dp", "ctx")


def _lin(x, y, z, c):
    return ((x % NX) * NZ + z % NZ) * (NY * 2) + (y % NY) * 2 + c


def _pairs(move):
    return [
        (_lin(x, y, z, c), _lin(*move(x, y, z, c)))
        for x in range(NX)
        for z in range(NZ)
        for y in range(NY)
        for c in range(2)
    ]


Y_UP = _pairs(lambda x, y, z, c: (x, y + 1, z, c))
Y_DN = _pairs(lambda x, y, z, c: (x, y - 1, z, c))
Y_TWO = _pairs(lambda x, y, z, c: (x, y + 2, z, c))
Y_FWD = _pairs(lambda x, y, z, c: (x, y + 1 - 2 * c, z, c))
Y_REV = _pairs(lambda x, y, z, c: (x, y - 1 + 2 * c, z, c))
X_FWD = _pairs(lambda x, y, z, c: (x + 1 - 2 * c, y, z, c))
X_REV = _pairs(lambda x, y, z, c: (x - 1 + 2 * c, y, z, c))
X_TWO = _pairs(lambda x, y, z, c: (x + 2, y, z, c))
SWAP = _pairs(lambda x, y, z, c: (x, y, z, 1 - c))
Z_OUT = [_pairs(lambda x, y, z, c, j=j: (x, y, z + j if c == 0 else z - 1 - j, c)) for j in range(4)]
Z_BACK = [_pairs(lambda x, y, z, c, j=j: (x, y, z - j if c == 0 else z + 1 + j, c)) for j in range(2)]
Z_BACK_ACROSS = [
    _pairs(lambda x, y, z, c, j=j: (x, y, z - j if c == 0 else z + 1 + j, 1 - c)) for j in range(2)
]
Z_PAIR_BACK = _pairs(lambda x, y, z, c: (x, y, z - 2 + 4 * c, c))


def send(value, pairs):
    return lax.ppermute(value, AXES, pairs)


def column_of(z, c, j):
    return lax.rem(jnp.where(c == 0, z + NZ - j, z + 1 + j), NZ)


HBM = pl.BlockSpec(memory_space=pltpu.HBM)
VMEM = pl.BlockSpec(memory_space=pltpu.VMEM)
SDS = jax.ShapeDtypeStruct
PAIR = SDS((2, HD, ENC_D), BF)
SOLO = SDS((1, HD, ENC_D), BF)
ROWS = SDS((SLOTS, NBL, ENC_D), BF)
HEAD_OUT = SDS((2, 4, 128, HD), BF)
TOKENS = SLOTS * NBL


def params(mib):
    return pltpu.CompilerParams(vmem_limit_bytes=mib * 1024 * 1024)


def dot(a, b, dims):
    return lax.dot_general(a, b, (dims, ((), ())), preferred_element_type=F32)


def scratch(shape, dtype=BF):
    return pltpu.VMEM(shape, dtype)


def slot_value(ids, pids, which, s):
    index = which * 4 + lax.rem(s, 4) if not isinstance(s, int) else which * 4 + s % 4
    return jnp.where(s < 4, ids[index], pids[index])


def fetch_rows(pos, ids, pids, sources, rows, sem):
    y, c = pos[1], pos[3]

    def fetch(s, carry):
        owner = slot_value(ids, pids, 0, s)
        row = slot_value(ids, pids, 1, s)
        away = lax.rem(owner // 2 + NY - y, NY)
        other = lax.rem(owner, 2) != c
        for side in range(2):
            here = other if side else jnp.logical_not(other)
            core = 1 - c if side else c
            own, fwd, rev, far = sources[4 * side:4 * side + 4]
            for place, buf in ((0, own), (3 - 2 * core, fwd), (1 + 2 * core, rev), (2, far)):
                @pl.when(jnp.logical_and(here, away == place))
                def _():
                    pltpu.make_async_copy(buf.at[row], rows.at[s], sem.at[s]).start()
        return carry

    lax.fori_loop(0, SLOTS, fetch, 0)


def fetch_weights(pos, own, fwd, rev, far, weight, sem):
    c = pos[3]
    for xx in range(NX):
        away = lax.rem(xx + NX - pos[0], NX)
        place = (xx % 2) * 2 + xx // 2
        for j in range(2):
            for value, src in ((0, own), (3 - 2 * c, fwd), (1 + 2 * c, rev), (2, far)):
                @pl.when(away == value)
                def _():
                    pltpu.make_async_copy(src.at[j], weight.at[j, place], sem.at[j]).start()


def fetch_heads(pos, first, arrays, amat, sem):
    amat[:, :, 0:GROUP, HD:] = jnp.zeros((4, 4, GROUP, HD), BF)
    amat[:, :, GROUP:, 0:HD] = jnp.zeros((4, 4, GROUP, HD), BF)
    for j in range(2):
        col = column_of(pos[2], pos[3], first + j)
        for hi in range(2):
            lanes = pl.ds(pl.multiple_of((hi * NZ + col) * HD, HD), HD)
            for part in range(2):
                for kind in range(2):
                    src = arrays[part].at[kind, :, :, lanes]
                    there = pl.ds(2 * part, 2), pl.ds(kind * GROUP, GROUP), pl.ds(kind * HD, HD)
                    pltpu.make_async_copy(src, amat.at[2 * j + hi, there[0], there[1], there[2]], sem).start()


def wait_heads(amat, sem):
    half = amat.at[:, :, 0:GROUP]
    pltpu.make_async_copy(half, half, sem).wait()


def bundle_math(ids, pids, rows, weight, w_sem, amat, kv, grad, heads, q_sem):
    scale = HD ** -0.5
    lane = lax.broadcasted_iota(jnp.int32, (GROUP, 2 * NBL), 1)
    live = []
    for g in range(4):
        live0 = NBL - slot_value(ids, pids, 2, 2 * g)
        live1 = NBL - slot_value(ids, pids, 2, 2 * g + 1)
        live.append(lane < jnp.where(lane < NBL, live0, live1 + NBL))
    for j in range(2):
        pltpu.make_async_copy(weight.at[j], weight.at[j], w_sem.at[j]).wait()
        enc = rows[...].reshape(TOKENS, ENC_D)
        kv[j] = dot(enc, weight[j].reshape(512, ENC_D), ((1,), (1,))).astype(BF)
    wait_heads(amat, q_sem)

    def begin(j, g, hi):
        both = kv[j, g * 256:(g + 1) * 256, hi * 256:(hi + 1) * 256]
        mat = amat[2 * j + hi, g]
        return both, mat, dot(mat, both, ((1,), (1,)))

    steps = [(j, g, hi) for j in range(2) for g in range(4) for hi in range(2)]
    ahead = begin(*steps[0])
    for n, (j, g, hi) in enumerate(steps):
        both, mat, sd = ahead
        if n + 1 < len(steps):
            ahead = begin(*steps[n + 1])
        s = jnp.where(live[g], sd[:GROUP] * scale, NEG)
        e = jnp.exp(s - jnp.max(s, axis=1, keepdims=True))
        p = e * (1.0 / jnp.sum(e, axis=1, keepdims=True))
        dp = sd[GROUP:]
        delta = jnp.sum(p * dp, axis=1, keepdims=True)
        ds = p * (dp - delta) * scale
        pm = jnp.concatenate([ds.astype(BF), p.astype(BF)], axis=0)
        out = dot(pm, both, ((1,), (0,)))
        spot = pl.ds((g % 2) * GROUP, GROUP)
        heads[g // 2, 0, 2 * j + hi, spot] = out[GROUP:, HD:].astype(BF)
        heads[g // 2, 1, 2 * j + hi, spot] = out[:GROUP, :HD].astype(BF)
        cols = j * 512 + hi * 256
        grad[g * 256:(g + 1) * 256, cols:cols + 256] = dot(pm, mat, ((0,), (0,))).astype(BF)


def back_terms(grad, weight, terms, terms_out, sem, before=None):
    for t in range(4):
        total = dot(grad[t * 256:(t + 1) * 256], weight[...].reshape(1024, ENC_D), ((1,), (0,)))
        if before is not None:
            total = total + before[2 * t:2 * t + 2].reshape(256, ENC_D).astype(F32)
        terms[2 * t:2 * t + 2] = total.astype(BF).reshape(2, NBL, ENC_D)
        here = pl.ds(2 * t, 2)
        pltpu.make_async_copy(terms.at[here], terms_out.at[here], sem).start()


def weight_products(pos, grad, rows, parts):
    for j in range(2):
        for hi in range(2):
            cols = j * 512 + hi * 256
            product = dot(
                grad[:, cols:cols + 256], rows[...].reshape(TOKENS, ENC_D), ((0,), (0,))
            ).astype(BF)
            for kind in range(2):
                away = lax.rem(2 * kind + hi + NX - pos[0], NX)
                parts[away, j] = product[kind * HD:(kind + 1) * HD]


def part_copies(pos, parts, outs, sem):
    own, fwd, rev, far = outs
    c = pos[3]
    pairs = (
        (parts.at[2], far),
        (parts.at[3 - 2 * c], rev),
        (parts.at[1 + 2 * c], fwd),
        (parts.at[0], own),
    )
    return [pltpu.make_async_copy(src, dst, sem.at[n]) for n, (src, dst) in enumerate(pairs)]


PART_OUTS = (PAIR,) * 4


def bundle_kernel(
    base, pos, ids, pids, row_sources, before_in, weights, arrays, terms_out, own_out, par_out, part_outs, rows_out,
    rows, weight, amat, kv, grad, heads, terms, parts, row_sem, w_sem, q_sem, sem, part_sem, before,
):
    copies = []
    if base:
        fetch_rows(pos, ids, pids, row_sources, rows, row_sem)
    else:
        for s in range(SLOTS):
            pltpu.make_async_copy(row_sources[0].at[s], rows.at[s], row_sem.at[s]).start()
        before_copy = pltpu.make_async_copy(before_in, before, sem.at[4])
        before_copy.start()
    fetch_weights(pos, *weights, weight, w_sem)
    fetch_heads(pos, base, arrays, amat, q_sem)
    for s in range(SLOTS):
        pltpu.make_async_copy(rows.at[s], rows.at[s], row_sem.at[s]).wait()
    if base:
        copies.append(pltpu.make_async_copy(rows, rows_out, sem.at[0]))
        copies[-1].start()
    bundle_math(ids, pids, rows, weight, w_sem, amat, kv, grad, heads, q_sem)
    for n, out in enumerate((own_out, par_out)):
        copies.append(pltpu.make_async_copy(heads.at[n], out, sem.at[1 + n]))
        copies[-1].start()
    if base:
        weight_products(pos, grad, rows, parts)
        outs = part_copies(pos, parts, part_outs, part_sem)
        for copy in outs:
            copy.start()
        back_terms(grad, weight, terms, terms_out, sem.at[3])
    else:
        before_copy.wait()
        back_terms(grad, weight, terms, terms_out, sem.at[3], before)
    copies.append(pltpu.make_async_copy(terms, terms_out, sem.at[3]))
    if not base:
        weight_products(pos, grad, rows, parts)
        outs = part_copies(pos, parts, part_outs, part_sem)
        for copy in outs:
            copy.start()
    for copy in copies + outs:
        copy.wait()


def first_kernel(pos, ids, pids, *refs):
    sources, weights, arrays, refs = refs[:8], refs[8:12], refs[12:14], refs[14:]
    rows_out, terms_out, own_out, par_out, refs = *refs[:4], refs[4:]
    part_outs, refs = refs[:4], refs[4:]
    bundle_kernel(
        2, pos, ids, pids, sources, None, weights, arrays, terms_out, own_out, par_out, part_outs, rows_out, *refs, None
    )


def second_kernel(pos, ids, pids, *refs):
    sources, before_in, weights, arrays, refs = refs[:1], refs[1], refs[2:6], refs[6:8], refs[8:]
    terms_out, own_out, par_out, refs = *refs[:3], refs[3:]
    part_outs, refs = refs[:4], refs[4:]
    bundle_kernel(
        0, pos, ids, pids, sources, before_in, weights, arrays, terms_out, own_out, par_out, part_outs, None, *refs
    )


def bundle(kernel, name, out_shape, extra, pos, ids, pids, *arrays):
    return pl.pallas_call(
        kernel,
        out_shape=out_shape,
        grid_spec=pltpu.PrefetchScalarGridSpec(
            num_scalar_prefetch=3,
            grid=(),
            in_specs=[HBM] * len(arrays),
            out_specs=[HBM] * len(out_shape),
            scratch_shapes=[
                scratch((SLOTS, NBL, ENC_D)),
                scratch((2, 4, HD, ENC_D)),
                scratch((4, 4, 128, 256)),
                scratch((2, TOKENS, 512)),
                scratch((TOKENS, 1024)),
                scratch((2, 2, 4, 128, HD)),
                scratch((SLOTS, NBL, ENC_D)),
                scratch((4, 2, HD, ENC_D)),
                pltpu.SemaphoreType.DMA((SLOTS,)),
                pltpu.SemaphoreType.DMA((2,)),
                pltpu.SemaphoreType.DMA,
                pltpu.SemaphoreType.DMA((5,)),
                pltpu.SemaphoreType.DMA((4,)),
            ] + extra,
        ),
        compiler_params=params(60),
        cost_estimate=pl.CostEstimate(flops=6_000_000_000, bytes_accessed=16_000_000, transcendentals=300_000),
        name=name,
    )(pos, ids, pids, *arrays)


def first(*args):
    return bundle(first_kernel, "first_heads", (ROWS, ROWS, HEAD_OUT, HEAD_OUT) + PART_OUTS, [], *args)


def second(*args):
    return bundle(
        second_kernel, "second_heads", (ROWS, HEAD_OUT, HEAD_OUT) + PART_OUTS, [scratch((SLOTS, NBL, ENC_D))], *args
    )


def near_kernel(pos, *refs):
    values, outs = refs[:4], refs[4:]
    c = pos[3]
    for j in range(2):
        total = values[0][j].astype(F32)
        for value in values[1:]:
            total = total + value[j].astype(F32)
        total = total.astype(BF)
        low, high = total[:64], total[64:]
        outs[j][...] = jnp.where(c == 0, low, high)
        outs[2 + j][...] = jnp.where(c == 0, high, low)


def near_halves(pos, *values):
    return pl.pallas_call(
        near_kernel,
        out_shape=(SDS((64, ENC_D), BF),) * 4,
        grid_spec=pltpu.PrefetchScalarGridSpec(
            num_scalar_prefetch=1, grid=(), in_specs=[VMEM] * 4, out_specs=[VMEM] * 4
        ),
        compiler_params=params(16),
        cost_estimate=pl.CostEstimate(flops=1_000_000, bytes_accessed=2_500_000, transcendentals=0),
        name="near_halves",
    )(pos, *values)


def route_kernel(pos, ids, pids, terms, p_terms, own, fwd, rev, far, total):
    y, c = pos[1], pos[3]
    total[...] = jnp.zeros_like(total)
    for s in range(SLOTS):
        src = ids if s < 4 else pids
        owner, row = src[s % 4], src[4 + s % 4]

        @pl.when(lax.rem(owner, 2) == c)
        def _():
            place = lax.rem(owner // 2 + NY - y, NY) * 4 + row
            total[place] = total[place] + (terms[s].astype(F32) + p_terms[s ^ 4].astype(F32))

    far[...] = total[8:12].astype(BF)
    rev[...] = total[pl.ds(12 - 8 * c, 4)].astype(BF)
    fwd[...] = total[pl.ds(4 + 8 * c, 4)].astype(BF)
    own[...] = total[0:4].astype(BF)


def route(pos, ids, pids, terms, p_terms):
    return pl.pallas_call(
        route_kernel,
        out_shape=(SDS((4, NBL, ENC_D), BF),) * 4,
        grid_spec=pltpu.PrefetchScalarGridSpec(
            num_scalar_prefetch=3,
            grid=(),
            in_specs=[VMEM] * 2,
            out_specs=[VMEM] * 4,
            scratch_shapes=[scratch((16, NBL, ENC_D), F32)],
        ),
        compiler_params=params(40),
        cost_estimate=pl.CostEstimate(flops=10_000_000, bytes_accessed=8_000_000, transcendentals=0),
        name="route",
    )(pos, ids, pids, terms, p_terms)


def join_kernel(pos, own_a, own_b, got_a, got_b, att_out, dq_out):
    z, c = pos[2], pos[3]
    for j in range(4):
        for core, (a, b) in ((c, (own_a, own_b)), (1 - c, (got_a, got_b))):
            src = b if j < 2 else a
            col = column_of(z, core, j)
            for hi in range(2):
                lanes = pl.ds(pl.multiple_of((hi * NZ + col) * HD, HD), HD)
                att_out[:, lanes] = src[0, 2 * (j % 2) + hi]
                dq_out[:, lanes] = src[1, 2 * (j % 2) + hi]


def join(pos, *arrays):
    return pl.pallas_call(
        join_kernel,
        out_shape=(SDS((128, HQ), BF),) * 2,
        grid_spec=pltpu.PrefetchScalarGridSpec(
            num_scalar_prefetch=1, grid=(), in_specs=[VMEM] * 4, out_specs=[VMEM] * 2
        ),
        compiler_params=params(16),
        cost_estimate=pl.CostEstimate(flops=0, bytes_accessed=4_000_000, transcendentals=0),
        name="join",
    )(pos, *arrays)


def add(*values):
    total = values[0].astype(F32)
    for value in values[1:]:
        total = total + value.astype(F32)
    return total


def tie(*values):
    return lax.optimization_barrier(values)


def on_device(queries, encodings, weight, shard, row, pad, cotangent):
    dp, ctx = lax.axis_index("dp"), lax.axis_index("ctx")
    pos = jnp.stack([dp // NZ, ctx // 2, dp % NZ, ctx % 2]).astype(jnp.int32)
    core = ctx % 2
    ids = jnp.concatenate([shard.reshape(4), row.reshape(4), pad.reshape(4)])
    q = queries.reshape(128, HQ)
    cot = cotangent.reshape(128, HQ)
    enc = encodings.reshape(4, NBL, ENC_D)

    y1, y2, p_own, pids = send(enc, Y_FWD), send(enc, Y_REV), send(enc, SWAP), send(ids, SWAP)
    u3, u2 = send(weight, Z_OUT[3]), send(weight, Z_OUT[2])
    ua = jnp.stack([u2, u3])
    ua, y1, y2, p_own, pids, weight_2 = tie(ua, y1, y2, p_own, pids, weight)
    a1, a2, y3 = send(ua, X_FWD), send(ua, X_REV), send(y1, Y_FWD)
    u1, u0 = send(weight_2, Z_OUT[1]), send(weight_2, Z_OUT[0])
    ub = jnp.stack([u0, u1])
    heads_in = jnp.stack([q, cot]).reshape(2, 2, GROUP, HQ)
    a1, a2, ub, y1, y2, heads_in = tie(a1, a2, ub, y1, y2, heads_in)
    a3, heads_par = send(a1, X_FWD), send(heads_in, SWAP)
    p_y1, p_y2 = send(y1, SWAP), send(y2, SWAP)
    y3, a3 = tie(y3, a3)
    p_y3 = send(y3, SWAP)
    a3, p_y1, p_y2, p_y3, heads_par, ub = tie(a3, p_y1, p_y2, p_y3, heads_par, ub)
    b1, b2, b3 = send(ub, X_FWD), send(ub, X_REV), send(ub, X_TWO)

    rows, terms_a, own_a, par_a, *parts_a = first(
        pos, ids, pids, enc, y1, y2, y3, p_own, p_y1, p_y2, p_y3, ua, a1, a2, a3, heads_in, heads_par
    )
    got_a = send(par_a, SWAP)
    ga_own, ga_fwd, ga_rev, ga_far = parts_a
    ga1, ga2 = send(ga_far, X_FWD), send(ga_rev, X_REV)
    terms, own_b, par_b, gb_own, gb_fwd, gb_rev, gb_far = second(
        pos, ids, pids, rows, terms_a, ub, b1, b2, b3, heads_in, heads_par
    )
    terms, ga1, ga2, got_a = tie(terms, ga1, ga2, got_a)
    p_terms = send(terms, SWAP)
    ga3 = send(add(ga_fwd, ga1).astype(BF), X_FWD)
    gb1 = send(gb_far, X_FWD)
    e_own, e_fwd, e_rev, e_far = route(pos, ids, pids, terms, p_terms)
    e1 = send(e_far, Y_FWD)
    ga3, gb1, gb_rev, _ = tie(ga3, gb1, gb_rev, e_far)
    far = send(add(ga_own, ga2, ga3).astype(BF), Z_PAIR_BACK)
    gb3 = send(add(gb_fwd, gb1).astype(BF), X_FWD)
    gb2 = send(gb_rev, X_REV)
    e2 = send(e_rev, Y_REV)
    gb2, gb3, far, e1, e2 = tie(gb2, gb3, far, e1, e2)
    e3 = send(add(e_fwd, e1).astype(BF), Y_FWD)
    s0, s1, t0, t1 = near_halves(pos, gb_own, gb2, gb3, far)
    s0, s1 = send(s0, Z_BACK[0]), send(s1, Z_BACK[1])
    t0, t1 = send(t0, Z_BACK_ACROSS[0]), send(t1, Z_BACK_ACROSS[1])
    s0, s1, t0, t1, par_b, e3 = tie(s0, s1, t0, t1, par_b, e3)
    half = add(s0, s1, t0, t1).astype(BF)
    got_b = send(par_b, SWAP)
    half = add(half, send(half, Y_UP), send(half, Y_DN), send(half, Y_TWO))
    rest = send(half, SWAP)
    low = jnp.where(core == 0, half, rest)
    high = jnp.where(core == 0, rest, half)
    weight_gradient = jnp.concatenate([low, high])

    enc_grad = add(e_own, e2, e3).astype(BF)
    att, dq = join(pos, own_a, own_b, got_a, got_b)
    return (
        att.reshape(1, 128, HQ),
        dq.reshape(1, 128, HQ),
        enc_grad.reshape(1, 4, NBL, ENC_D),
        weight_gradient,
    )


def solution(mesh):
    rows = P("dp", "ctx", None)
    return jax.shard_map(
        on_device,
        mesh=mesh,
        in_specs=(rows, P("dp", "ctx", None, None), P("dp", None), rows, rows, rows, rows),
        out_specs=(rows, rows, P("dp", "ctx", None, None), P("dp", None)),
        check_vma=False,
    )
```

```python
import functools

import jax
import jax.numpy as jnp
from jax import lax
from jax.experimental import pallas as pl
from jax.experimental.pallas import tpu as pltpu
from jax.sharding import PartitionSpec as P

HEADS = 16
HD = 128
ENC_D = 896
NBL = 128
GROUP = 64
HQ = 2048
NX, NY, NZ = 4, 4, 8
SLOTS = 8
NEG = -1e30
BF = jnp.bfloat16
F32 = jnp.float32
AXES = ("dp", "ctx")


def _lin(x, y, z, c):
    return ((x % NX) * NZ + z % NZ) * (NY * 2) + (y % NY) * 2 + c


def _pairs(move):
    return [
        (_lin(x, y, z, c), _lin(*move(x, y, z, c)))
        for x in range(NX)
        for z in range(NZ)
        for y in range(NY)
        for c in range(2)
    ]


Y_UP = _pairs(lambda x, y, z, c: (x, y + 1, z, c))
Y_DN = _pairs(lambda x, y, z, c: (x, y - 1, z, c))
Y_TWO = _pairs(lambda x, y, z, c: (x, y + 2, z, c))
Y_FWD = _pairs(lambda x, y, z, c: (x, y + 1 - 2 * c, z, c))
Y_REV = _pairs(lambda x, y, z, c: (x, y - 1 + 2 * c, z, c))
X_FWD = _pairs(lambda x, y, z, c: (x + 1 - 2 * c, y, z, c))
X_REV = _pairs(lambda x, y, z, c: (x - 1 + 2 * c, y, z, c))
X_TWO = _pairs(lambda x, y, z, c: (x + 2, y, z, c))
SWAP = _pairs(lambda x, y, z, c: (x, y, z, 1 - c))
Z_OUT = [_pairs(lambda x, y, z, c, j=j: (x, y, z + j if c == 0 else z - 1 - j, c)) for j in range(4)]
Z_BACK = [_pairs(lambda x, y, z, c, j=j: (x, y, z - j if c == 0 else z + 1 + j, c)) for j in range(2)]
Z_BACK_ACROSS = [
    _pairs(lambda x, y, z, c, j=j: (x, y, z - j if c == 0 else z + 1 + j, 1 - c)) for j in range(2)
]
Z_PAIR_BACK = _pairs(lambda x, y, z, c: (x, y, z - 2 + 4 * c, c))


def send(value, pairs):
    return lax.ppermute(value, AXES, pairs)


def column_of(z, c, j):
    return lax.rem(jnp.where(c == 0, z + NZ - j, z + 1 + j), NZ)


HBM = pl.BlockSpec(memory_space=pltpu.HBM)
VMEM = pl.BlockSpec(memory_space=pltpu.VMEM)
SDS = jax.ShapeDtypeStruct
PAIR = SDS((2, HD, ENC_D), BF)
SOLO = SDS((1, HD, ENC_D), BF)
ROWS = SDS((SLOTS, NBL, ENC_D), BF)
HEAD_OUT = SDS((2, 4, 128, HD), BF)
TOKENS = SLOTS * NBL


def params(mib):
    return pltpu.CompilerParams(vmem_limit_bytes=mib * 1024 * 1024)


def dot(a, b, dims):
    return lax.dot_general(a, b, (dims, ((), ())), preferred_element_type=F32)


def scratch(shape, dtype=BF):
    return pltpu.VMEM(shape, dtype)


def slot_value(ids, pids, which, s):
    index = which * 4 + lax.rem(s, 4) if not isinstance(s, int) else which * 4 + s % 4
    return jnp.where(s < 4, ids[index], pids[index])


def fetch_rows(pos, ids, pids, sources, rows, sem):
    y, c = pos[1], pos[3]

    def fetch(s, carry):
        owner = slot_value(ids, pids, 0, s)
        row = slot_value(ids, pids, 1, s)
        away = lax.rem(owner // 2 + NY - y, NY)
        other = lax.rem(owner, 2) != c
        for side in range(2):
            here = other if side else jnp.logical_not(other)
            core = 1 - c if side else c
            own, fwd, rev, far = sources[4 * side:4 * side + 4]
            for place, buf in ((0, own), (3 - 2 * core, fwd), (1 + 2 * core, rev), (2, far)):
                @pl.when(jnp.logical_and(here, away == place))
                def _():
                    pltpu.make_async_copy(buf.at[row], rows.at[s], sem.at[s]).start()
        return carry

    lax.fori_loop(0, SLOTS, fetch, 0)


def fetch_weights(pos, own, fwd, rev, far, weight, sem):
    c = pos[3]
    for xx in range(NX):
        away = lax.rem(xx + NX - pos[0], NX)
        place = (xx % 2) * 2 + xx // 2
        for j in range(2):
            for value, src in ((0, own), (3 - 2 * c, fwd), (1 + 2 * c, rev), (2, far)):
                @pl.when(away == value)
                def _():
                    pltpu.make_async_copy(src.at[j], weight.at[j, place], sem.at[j]).start()


def fetch_heads(pos, first, arrays, amat, sem):
    amat[:, :, 0:GROUP, HD:] = jnp.zeros((4, 4, GROUP, HD), BF)
    amat[:, :, GROUP:, 0:HD] = jnp.zeros((4, 4, GROUP, HD), BF)
    for j in range(2):
        col = column_of(pos[2], pos[3], first + j)
        for hi in range(2):
            lanes = pl.ds(pl.multiple_of((hi * NZ + col) * HD, HD), HD)
            for part in range(2):
                for kind in range(2):
                    src = arrays[part].at[kind, :, :, lanes]
                    there = pl.ds(2 * part, 2), pl.ds(kind * GROUP, GROUP), pl.ds(kind * HD, HD)
                    pltpu.make_async_copy(src, amat.at[2 * j + hi, there[0], there[1], there[2]], sem).start()


def wait_heads(amat, sem):
    half = amat.at[:, :, 0:GROUP]
    pltpu.make_async_copy(half, half, sem).wait()


def bundle_math(ids, pids, rows, weight, w_sem, amat, kv, grad, heads, q_sem):
    scale = HD ** -0.5
    lane = lax.broadcasted_iota(jnp.int32, (GROUP, 2 * NBL), 1)
    live = []
    for g in range(4):
        live0 = NBL - slot_value(ids, pids, 2, 2 * g)
        live1 = NBL - slot_value(ids, pids, 2, 2 * g + 1)
        live.append(lane < jnp.where(lane < NBL, live0, live1 + NBL))
    for j in range(2):
        pltpu.make_async_copy(weight.at[j], weight.at[j], w_sem.at[j]).wait()
        enc = rows[...].reshape(TOKENS, ENC_D)
        kv[j] = dot(enc, weight[j].reshape(512, ENC_D), ((1,), (1,))).astype(BF)
    wait_heads(amat, q_sem)

    def begin(j, g, hi):
        both = kv[j, g * 256:(g + 1) * 256, hi * 256:(hi + 1) * 256]
        mat = amat[2 * j + hi, g]
        return both, mat, dot(mat, both, ((1,), (1,)))

    steps = [(j, g, hi) for j in range(2) for g in range(4) for hi in range(2)]
    ahead = begin(*steps[0])
    for n, (j, g, hi) in enumerate(steps):
        both, mat, sd = ahead
        if n + 1 < len(steps):
            ahead = begin(*steps[n + 1])
        s = jnp.where(live[g], sd[:GROUP] * scale, NEG)
        e = jnp.exp(s - jnp.max(s, axis=1, keepdims=True))
        p = e * (1.0 / jnp.sum(e, axis=1, keepdims=True))
        dp = sd[GROUP:]
        delta = jnp.sum(p * dp, axis=1, keepdims=True)
        ds = p * (dp - delta) * scale
        pm = jnp.concatenate([ds.astype(BF), p.astype(BF)], axis=0)
        out = dot(pm, both, ((1,), (0,)))
        spot = pl.ds((g % 2) * GROUP, GROUP)
        heads[g // 2, 0, 2 * j + hi, spot] = out[GROUP:, HD:].astype(BF)
        heads[g // 2, 1, 2 * j + hi, spot] = out[:GROUP, :HD].astype(BF)
        cols = j * 512 + hi * 256
        grad[g * 256:(g + 1) * 256, cols:cols + 256] = dot(pm, mat, ((0,), (0,))).astype(BF)


def back_terms(grad, weight, terms, terms_out, sem, before=None):
    for t in range(4):
        total = dot(grad[t * 256:(t + 1) * 256], weight[...].reshape(1024, ENC_D), ((1,), (0,)))
        if before is not None:
            total = total + before[2 * t:2 * t + 2].reshape(256, ENC_D).astype(F32)
        terms[2 * t:2 * t + 2] = total.astype(BF).reshape(2, NBL, ENC_D)
        here = pl.ds(2 * t, 2)
        pltpu.make_async_copy(terms.at[here], terms_out.at[here], sem).start()


def weight_products(pos, grad, rows, parts):
    for j in range(2):
        for hi in range(2):
            cols = j * 512 + hi * 256
            product = dot(
                grad[:, cols:cols + 256], rows[...].reshape(TOKENS, ENC_D), ((0,), (0,))
            ).astype(BF)
            for kind in range(2):
                away = lax.rem(2 * kind + hi + NX - pos[0], NX)
                parts[away, j] = product[kind * HD:(kind + 1) * HD]


def part_copies(pos, parts, outs, sem):
    own, fwd, rev, far = outs
    c = pos[3]
    pairs = (
        (parts.at[2], far),
        (parts.at[3 - 2 * c], rev),
        (parts.at[1 + 2 * c], fwd),
        (parts.at[0], own),
    )
    return [pltpu.make_async_copy(src, dst, sem.at[n]) for n, (src, dst) in enumerate(pairs)]


PART_OUTS = (PAIR,) * 4


def bundle_kernel(
    base, pos, ids, pids, row_sources, weights, arrays, own_out, par_out, terms_out, part_outs, rows_out, grad_out,
    rows, weight, amat, kv, grad, heads, terms, parts, row_sem, w_sem, q_sem, sem, part_sem,
):
    copies = []
    if base:
        fetch_rows(pos, ids, pids, row_sources, rows, row_sem)
    else:
        for s in range(SLOTS):
            pltpu.make_async_copy(row_sources[0].at[s], rows.at[s], row_sem.at[s]).start()
    fetch_weights(pos, *weights, weight, w_sem)
    fetch_heads(pos, base, arrays, amat, q_sem)
    for s in range(SLOTS):
        pltpu.make_async_copy(rows.at[s], rows.at[s], row_sem.at[s]).wait()
    if base:
        copies.append(pltpu.make_async_copy(rows, rows_out, sem.at[0]))
        copies[-1].start()
    bundle_math(ids, pids, rows, weight, w_sem, amat, kv, grad, heads, q_sem)
    for n, out in enumerate((own_out, par_out)):
        copies.append(pltpu.make_async_copy(heads.at[n], out, sem.at[1 + n]))
        copies[-1].start()
    if base:
        weight_products(pos, grad, rows, parts)
        outs = part_copies(pos, parts, part_outs, part_sem)
        for copy in outs:
            copy.start()
        copies += outs
        back_terms(grad, weight, terms, terms_out, sem.at[3])
        copies.append(pltpu.make_async_copy(terms, terms_out, sem.at[3]))
    else:
        copies.append(pltpu.make_async_copy(grad, grad_out, sem.at[4]))
        copies[-1].start()
    for copy in copies:
        copy.wait()


def first_kernel(pos, ids, pids, *refs):
    sources, weights, arrays, refs = refs[:8], refs[8:12], refs[12:14], refs[14:]
    rows_out, terms_out, own_out, par_out, refs = *refs[:4], refs[4:]
    part_outs, refs = refs[:4], refs[4:]
    bundle_kernel(
        2, pos, ids, pids, sources, weights, arrays, own_out, par_out, terms_out, part_outs, rows_out, None, *refs
    )


def second_kernel(pos, ids, pids, *refs):
    sources, weights, arrays, refs = refs[:1], refs[1:5], refs[5:7], refs[7:]
    own_out, par_out, grad_out, refs = *refs[:3], refs[3:]
    bundle_kernel(
        0, pos, ids, pids, sources, weights, arrays, own_out, par_out, None, None, None, grad_out, *refs
    )


def third_kernel(pos, *refs):
    grad_in, rows_in, before_in, weights, refs = *refs[:3], refs[3:7], refs[7:]
    terms_out, part_outs, refs = refs[0], refs[1:5], refs[5:]
    grad, rows, before, weight, terms, parts, w_sem, sem, part_sem = refs
    loads = [
        pltpu.make_async_copy(grad_in, grad, sem.at[0]),
        pltpu.make_async_copy(rows_in, rows, sem.at[1]),
        pltpu.make_async_copy(before_in, before, sem.at[2]),
    ]
    for copy in loads:
        copy.start()
    fetch_weights(pos, *weights, weight, w_sem)
    loads[0].wait()
    loads[1].wait()
    weight_products(pos, grad, rows, parts)
    copies = part_copies(pos, parts, part_outs, part_sem)
    for copy in copies:
        copy.start()
    loads[2].wait()
    for j in range(2):
        pltpu.make_async_copy(weight.at[j], weight.at[j], w_sem.at[j]).wait()
    back_terms(grad, weight, terms, terms_out, sem.at[3], before)
    copies.append(pltpu.make_async_copy(terms, terms_out, sem.at[3]))
    for copy in copies:
        copy.wait()


def third(pos, *arrays):
    return pl.pallas_call(
        third_kernel,
        out_shape=(ROWS,) + PART_OUTS,
        grid_spec=pltpu.PrefetchScalarGridSpec(
            num_scalar_prefetch=1,
            grid=(),
            in_specs=[HBM] * len(arrays),
            out_specs=[HBM] * 5,
            scratch_shapes=[
                scratch((TOKENS, 1024)),
                scratch((SLOTS, NBL, ENC_D)),
                scratch((SLOTS, NBL, ENC_D)),
                scratch((2, 4, HD, ENC_D)),
                scratch((SLOTS, NBL, ENC_D)),
                scratch((4, 2, HD, ENC_D)),
                pltpu.SemaphoreType.DMA((2,)),
                pltpu.SemaphoreType.DMA((4,)),
                pltpu.SemaphoreType.DMA((4,)),
            ],
        ),
        compiler_params=params(60),
        cost_estimate=pl.CostEstimate(flops=4_000_000_000, bytes_accessed=12_000_000, transcendentals=0),
        name="third_products",
    )(pos, *arrays)


def bundle(kernel, name, out_shape, pos, ids, pids, *arrays):
    return pl.pallas_call(
        kernel,
        out_shape=out_shape,
        grid_spec=pltpu.PrefetchScalarGridSpec(
            num_scalar_prefetch=3,
            grid=(),
            in_specs=[HBM] * len(arrays),
            out_specs=[HBM] * len(out_shape),
            scratch_shapes=[
                scratch((SLOTS, NBL, ENC_D)),
                scratch((2, 4, HD, ENC_D)),
                scratch((4, 4, 128, 256)),
                scratch((2, TOKENS, 512)),
                scratch((TOKENS, 1024)),
                scratch((2, 2, 4, 128, HD)),
                scratch((SLOTS, NBL, ENC_D)),
                scratch((4, 2, HD, ENC_D)),
                pltpu.SemaphoreType.DMA((SLOTS,)),
                pltpu.SemaphoreType.DMA((2,)),
                pltpu.SemaphoreType.DMA,
                pltpu.SemaphoreType.DMA((5,)),
                pltpu.SemaphoreType.DMA((4,)),
            ],
        ),
        compiler_params=params(60),
        cost_estimate=pl.CostEstimate(flops=6_000_000_000, bytes_accessed=16_000_000, transcendentals=300_000),
        name=name,
    )(pos, ids, pids, *arrays)


def first(*args):
    return bundle(first_kernel, "first_heads", (ROWS, ROWS, HEAD_OUT, HEAD_OUT) + PART_OUTS, *args)


def second(*args):
    return bundle(second_kernel, "second_heads", (HEAD_OUT, HEAD_OUT, SDS((TOKENS, 1024), BF)), *args)


def near_kernel(pos, *refs):
    values, outs = refs[:4], refs[4:]
    c = pos[3]
    for j in range(2):
        total = values[0][j].astype(F32)
        for value in values[1:]:
            total = total + value[j].astype(F32)
        total = total.astype(BF)
        low, high = total[:64], total[64:]
        outs[j][...] = jnp.where(c == 0, low, high)
        outs[2 + j][...] = jnp.where(c == 0, high, low)


def near_halves(pos, *values):
    return pl.pallas_call(
        near_kernel,
        out_shape=(SDS((64, ENC_D), BF),) * 4,
        grid_spec=pltpu.PrefetchScalarGridSpec(
            num_scalar_prefetch=1, grid=(), in_specs=[VMEM] * 4, out_specs=[VMEM] * 4
        ),
        compiler_params=params(16),
        cost_estimate=pl.CostEstimate(flops=1_000_000, bytes_accessed=2_500_000, transcendentals=0),
        name="near_halves",
    )(pos, *values)


def route_kernel(pos, ids, pids, terms, p_terms, own, fwd, rev, far, total):
    y, c = pos[1], pos[3]
    total[...] = jnp.zeros_like(total)
    for s in range(SLOTS):
        src = ids if s < 4 else pids
        owner, row = src[s % 4], src[4 + s % 4]

        @pl.when(lax.rem(owner, 2) == c)
        def _():
            place = lax.rem(owner // 2 + NY - y, NY) * 4 + row
            total[place] = total[place] + (terms[s].astype(F32) + p_terms[s ^ 4].astype(F32))

    far[...] = total[8:12].astype(BF)
    rev[...] = total[pl.ds(12 - 8 * c, 4)].astype(BF)
    fwd[...] = total[pl.ds(4 + 8 * c, 4)].astype(BF)
    own[...] = total[0:4].astype(BF)


def route(pos, ids, pids, terms, p_terms):
    return pl.pallas_call(
        route_kernel,
        out_shape=(SDS((4, NBL, ENC_D), BF),) * 4,
        grid_spec=pltpu.PrefetchScalarGridSpec(
            num_scalar_prefetch=3,
            grid=(),
            in_specs=[VMEM] * 2,
            out_specs=[VMEM] * 4,
            scratch_shapes=[scratch((16, NBL, ENC_D), F32)],
        ),
        compiler_params=params(40),
        cost_estimate=pl.CostEstimate(flops=10_000_000, bytes_accessed=8_000_000, transcendentals=0),
        name="route",
    )(pos, ids, pids, terms, p_terms)


def join_kernel(pos, own_a, own_b, got_a, got_b, att_out, dq_out):
    z, c = pos[2], pos[3]
    for j in range(4):
        for core, (a, b) in ((c, (own_a, own_b)), (1 - c, (got_a, got_b))):
            src = b if j < 2 else a
            col = column_of(z, core, j)
            for hi in range(2):
                lanes = pl.ds(pl.multiple_of((hi * NZ + col) * HD, HD), HD)
                att_out[:, lanes] = src[0, 2 * (j % 2) + hi]
                dq_out[:, lanes] = src[1, 2 * (j % 2) + hi]


def join(pos, *arrays):
    return pl.pallas_call(
        join_kernel,
        out_shape=(SDS((128, HQ), BF),) * 2,
        grid_spec=pltpu.PrefetchScalarGridSpec(
            num_scalar_prefetch=1, grid=(), in_specs=[VMEM] * 4, out_specs=[VMEM] * 2
        ),
        compiler_params=params(16),
        cost_estimate=pl.CostEstimate(flops=0, bytes_accessed=4_000_000, transcendentals=0),
        name="join",
    )(pos, *arrays)


def add(*values):
    total = values[0].astype(F32)
    for value in values[1:]:
        total = total + value.astype(F32)
    return total


def tie(*values):
    return lax.optimization_barrier(values)


def on_device(queries, encodings, weight, shard, row, pad, cotangent):
    dp, ctx = lax.axis_index("dp"), lax.axis_index("ctx")
    pos = jnp.stack([dp // NZ, ctx // 2, dp % NZ, ctx % 2]).astype(jnp.int32)
    core = ctx % 2
    ids = jnp.concatenate([shard.reshape(4), row.reshape(4), pad.reshape(4)])
    q = queries.reshape(128, HQ)
    cot = cotangent.reshape(128, HQ)
    enc = encodings.reshape(4, NBL, ENC_D)

    y1, y2, p_own, pids = send(enc, Y_FWD), send(enc, Y_REV), send(enc, SWAP), send(ids, SWAP)
    u3, u2 = send(weight, Z_OUT[3]), send(weight, Z_OUT[2])
    ua = jnp.stack([u2, u3])
    ua, y1, y2, p_own, pids, weight_2 = tie(ua, y1, y2, p_own, pids, weight)
    a1, a2, y3 = send(ua, X_FWD), send(ua, X_REV), send(y1, Y_FWD)
    u1, u0 = send(weight_2, Z_OUT[1]), send(weight_2, Z_OUT[0])
    ub = jnp.stack([u0, u1])
    heads_in = jnp.stack([q, cot]).reshape(2, 2, GROUP, HQ)
    a1, a2, ub, y1, y2, heads_in = tie(a1, a2, ub, y1, y2, heads_in)
    a3, heads_par = send(a1, X_FWD), send(heads_in, SWAP)
    p_y1, p_y2 = send(y1, SWAP), send(y2, SWAP)
    y3, a3 = tie(y3, a3)
    p_y3 = send(y3, SWAP)
    a3, p_y1, p_y2, p_y3, heads_par, ub = tie(a3, p_y1, p_y2, p_y3, heads_par, ub)
    b1, b2, b3 = send(ub, X_FWD), send(ub, X_REV), send(ub, X_TWO)

    rows, terms_a, own_a, par_a, *parts_a = first(
        pos, ids, pids, enc, y1, y2, y3, p_own, p_y1, p_y2, p_y3, ua, a1, a2, a3, heads_in, heads_par
    )
    got_a = send(par_a, SWAP)
    ga_own, ga_fwd, ga_rev, ga_far = parts_a
    ga1, ga2 = send(ga_far, X_FWD), send(ga_rev, X_REV)
    own_b, par_b, grad = second(pos, ids, pids, rows, ub, b1, b2, b3, heads_in, heads_par)
    grad, ga1, ga2, got_a = tie(grad, ga1, ga2, got_a)
    ga3 = send(add(ga_fwd, ga1).astype(BF), X_FWD)
    terms, gb_own, gb_fwd, gb_rev, gb_far = third(pos, grad, rows, terms_a, ub, b1, b2, b3)
    terms, ga3 = tie(terms, ga3)
    p_terms = send(terms, SWAP)
    gb1, gb2 = send(gb_far, X_FWD), send(gb_rev, X_REV)
    far = send(add(ga_own, ga2, ga3).astype(BF), Z_PAIR_BACK)
    e_own, e_fwd, e_rev, e_far = route(pos, ids, pids, terms, p_terms)
    e1 = send(e_far, Y_FWD)
    gb1, gb2, far, _ = tie(gb1, gb2, far, e_far)
    gb3 = send(add(gb_fwd, gb1).astype(BF), X_FWD)
    e2 = send(e_rev, Y_REV)
    gb2, gb3, far, e1, e2 = tie(gb2, gb3, far, e1, e2)
    e3 = send(add(e_fwd, e1).astype(BF), Y_FWD)
    s0, s1, t0, t1 = near_halves(pos, gb_own, gb2, gb3, far)
    s0, s1 = send(s0, Z_BACK[0]), send(s1, Z_BACK[1])
    t0, t1 = send(t0, Z_BACK_ACROSS[0]), send(t1, Z_BACK_ACROSS[1])
    s0, s1, t0, t1, par_b, e3 = tie(s0, s1, t0, t1, par_b, e3)
    half = add(s0, s1, t0, t1).astype(BF)
    got_b = send(par_b, SWAP)
    half = add(half, send(half, Y_UP), send(half, Y_DN), send(half, Y_TWO))
    rest = send(half, SWAP)
    low = jnp.where(core == 0, half, rest)
    high = jnp.where(core == 0, rest, half)
    weight_gradient = jnp.concatenate([low, high])

    enc_grad = add(e_own, e2, e3).astype(BF)
    att, dq = join(pos, own_a, own_b, got_a, got_b)
    return (
        att.reshape(1, 128, HQ),
        dq.reshape(1, 128, HQ),
        enc_grad.reshape(1, 4, NBL, ENC_D),
        weight_gradient,
    )


def solution(mesh):
    rows = P("dp", "ctx", None)
    return jax.shard_map(
        on_device,
        mesh=mesh,
        in_specs=(rows, P("dp", "ctx", None, None), P("dp", None), rows, rows, rows, rows),
        out_specs=(rows, rows, P("dp", "ctx", None, None), P("dp", None)),
        check_vma=False,
    )
```

```python
import functools

import jax
import jax.numpy as jnp
from jax import lax
from jax.experimental import pallas as pl
from jax.experimental.pallas import tpu as pltpu
from jax.sharding import PartitionSpec as P

HEADS = 16
HD = 128
ENC_D = 896
NBL = 128
GROUP = 64
HQ = 2048
NX, NY, NZ = 4, 4, 8
SLOTS = 8
NEG = -1e30
BF = jnp.bfloat16
F32 = jnp.float32
AXES = ("dp", "ctx")


def _lin(x, y, z, c):
    return ((x % NX) * NZ + z % NZ) * (NY * 2) + (y % NY) * 2 + c


def _pairs(move):
    return [
        (_lin(x, y, z, c), _lin(*move(x, y, z, c)))
        for x in range(NX)
        for z in range(NZ)
        for y in range(NY)
        for c in range(2)
    ]


Y_UP = _pairs(lambda x, y, z, c: (x, y + 1, z, c))
Y_DN = _pairs(lambda x, y, z, c: (x, y - 1, z, c))
Y_TWO = _pairs(lambda x, y, z, c: (x, y + 2, z, c))
Y_FWD = _pairs(lambda x, y, z, c: (x, y + 1 - 2 * c, z, c))
Y_REV = _pairs(lambda x, y, z, c: (x, y - 1 + 2 * c, z, c))
X_FWD = _pairs(lambda x, y, z, c: (x + 1 - 2 * c, y, z, c))
X_REV = _pairs(lambda x, y, z, c: (x - 1 + 2 * c, y, z, c))
X_TWO = _pairs(lambda x, y, z, c: (x + 2, y, z, c))
SWAP = _pairs(lambda x, y, z, c: (x, y, z, 1 - c))
Z_OUT = [_pairs(lambda x, y, z, c, j=j: (x, y, z + j if c == 0 else z - 1 - j, c)) for j in range(4)]
Z_BACK = [_pairs(lambda x, y, z, c, j=j: (x, y, z - j if c == 0 else z + 1 + j, c)) for j in range(2)]
Z_BACK_ACROSS = [
    _pairs(lambda x, y, z, c, j=j: (x, y, z - j if c == 0 else z + 1 + j, 1 - c)) for j in range(2)
]
Z_PAIR_BACK = _pairs(lambda x, y, z, c: (x, y, z - 2 + 4 * c, c))


def send(value, pairs):
    return lax.ppermute(value, AXES, pairs)


def column_of(z, c, j):
    return lax.rem(jnp.where(c == 0, z + NZ - j, z + 1 + j), NZ)


HBM = pl.BlockSpec(memory_space=pltpu.HBM)
VMEM = pl.BlockSpec(memory_space=pltpu.VMEM)
SDS = jax.ShapeDtypeStruct
PAIR = SDS((2, HD, ENC_D), BF)
SOLO = SDS((1, HD, ENC_D), BF)
ROWS = SDS((SLOTS, NBL, ENC_D), BF)
HEAD_OUT = SDS((2, 4, 128, HD), BF)
TOKENS = SLOTS * NBL


def params(mib):
    return pltpu.CompilerParams(vmem_limit_bytes=mib * 1024 * 1024)


def dot(a, b, dims):
    return lax.dot_general(a, b, (dims, ((), ())), preferred_element_type=F32)


def scratch(shape, dtype=BF):
    return pltpu.VMEM(shape, dtype)


def slot_value(ids, pids, which, s):
    index = which * 4 + lax.rem(s, 4) if not isinstance(s, int) else which * 4 + s % 4
    return jnp.where(s < 4, ids[index], pids[index])


def fetch_rows(pos, ids, pids, sources, rows, sem):
    y, c = pos[1], pos[3]

    def fetch(s, carry):
        owner = slot_value(ids, pids, 0, s)
        row = slot_value(ids, pids, 1, s)
        away = lax.rem(owner // 2 + NY - y, NY)
        other = lax.rem(owner, 2) != c
        for side in range(2):
            here = other if side else jnp.logical_not(other)
            core = 1 - c if side else c
            own, fwd, rev, far = sources[4 * side:4 * side + 4]
            for place, buf in ((0, own), (3 - 2 * core, fwd), (1 + 2 * core, rev), (2, far)):
                @pl.when(jnp.logical_and(here, away == place))
                def _():
                    pltpu.make_async_copy(buf.at[row], rows.at[s], sem.at[s]).start()
        return carry

    lax.fori_loop(0, SLOTS, fetch, 0)


def fetch_weights(pos, own, fwd, rev, far, weight, sem):
    c = pos[3]
    for xx in range(NX):
        away = lax.rem(xx + NX - pos[0], NX)
        place = (xx % 2) * 2 + xx // 2
        for j in range(2):
            for value, src in ((0, own), (3 - 2 * c, fwd), (1 + 2 * c, rev), (2, far)):
                @pl.when(away == value)
                def _():
                    pltpu.make_async_copy(src.at[j], weight.at[j, place], sem.at[j]).start()


def fetch_heads(pos, first, arrays, amat, sem):
    amat[:, :, 0:GROUP, HD:] = jnp.zeros((4, 4, GROUP, HD), BF)
    amat[:, :, GROUP:, 0:HD] = jnp.zeros((4, 4, GROUP, HD), BF)
    for j in range(2):
        col = column_of(pos[2], pos[3], first + j)
        for hi in range(2):
            lanes = pl.ds(pl.multiple_of((hi * NZ + col) * HD, HD), HD)
            for part in range(2):
                for kind in range(2):
                    src = arrays[part].at[kind, :, :, lanes]
                    there = pl.ds(2 * part, 2), pl.ds(kind * GROUP, GROUP), pl.ds(kind * HD, HD)
                    pltpu.make_async_copy(src, amat.at[2 * j + hi, there[0], there[1], there[2]], sem).start()


def wait_heads(amat, sem):
    half = amat.at[:, :, 0:GROUP]
    pltpu.make_async_copy(half, half, sem).wait()


def bundle_math(ids, pids, rows, weight, w_sem, amat, kv, grad, heads, q_sem):
    scale = HD ** -0.5
    lane = lax.broadcasted_iota(jnp.int32, (GROUP, 2 * NBL), 1)
    live = []
    for g in range(4):
        live0 = NBL - slot_value(ids, pids, 2, 2 * g)
        live1 = NBL - slot_value(ids, pids, 2, 2 * g + 1)
        live.append(lane < jnp.where(lane < NBL, live0, live1 + NBL))
    for j in range(2):
        pltpu.make_async_copy(weight.at[j], weight.at[j], w_sem.at[j]).wait()
        enc = rows[...].reshape(TOKENS, ENC_D)
        kv[j] = dot(enc, weight[j].reshape(512, ENC_D), ((1,), (1,))).astype(BF)
    wait_heads(amat, q_sem)

    def begin(j, g, hi):
        both = kv[j, g * 256:(g + 1) * 256, hi * 256:(hi + 1) * 256]
        mat = amat[2 * j + hi, g]
        return both, mat, dot(mat, both, ((1,), (1,)))

    steps = [(j, g, hi) for j in range(2) for g in range(4) for hi in range(2)]
    ahead = begin(*steps[0])
    for n, (j, g, hi) in enumerate(steps):
        both, mat, sd = ahead
        if n + 1 < len(steps):
            ahead = begin(*steps[n + 1])
        s = jnp.where(live[g], sd[:GROUP] * scale, NEG)
        e = jnp.exp(s - jnp.max(s, axis=1, keepdims=True))
        p = e * (1.0 / jnp.sum(e, axis=1, keepdims=True))
        dp = sd[GROUP:]
        delta = jnp.sum(p * dp, axis=1, keepdims=True)
        ds = p * (dp - delta) * scale
        pm = jnp.concatenate([ds.astype(BF), p.astype(BF)], axis=0)
        out = dot(pm, both, ((1,), (0,)))
        spot = pl.ds((g % 2) * GROUP, GROUP)
        heads[g // 2, 0, 2 * j + hi, spot] = out[GROUP:, HD:].astype(BF)
        heads[g // 2, 1, 2 * j + hi, spot] = out[:GROUP, :HD].astype(BF)
        cols = j * 512 + hi * 256
        grad[g * 256:(g + 1) * 256, cols:cols + 256] = dot(pm, mat, ((0,), (0,))).astype(BF)


def back_terms(grad, weight, terms, terms_out, sem, before=None):
    for t in range(4):
        total = dot(grad[t * 256:(t + 1) * 256], weight[...].reshape(1024, ENC_D), ((1,), (0,)))
        if before is not None:
            total = total + before[2 * t:2 * t + 2].reshape(256, ENC_D).astype(F32)
        terms[2 * t:2 * t + 2] = total.astype(BF).reshape(2, NBL, ENC_D)
        here = pl.ds(2 * t, 2)
        pltpu.make_async_copy(terms.at[here], terms_out.at[here], sem).start()


def weight_products(pos, grad, rows, parts):
    for j in range(2):
        for hi in range(2):
            cols = j * 512 + hi * 256
            product = dot(
                grad[:, cols:cols + 256], rows[...].reshape(TOKENS, ENC_D), ((0,), (0,))
            ).astype(BF)
            for kind in range(2):
                away = lax.rem(2 * kind + hi + NX - pos[0], NX)
                parts[away, j] = product[kind * HD:(kind + 1) * HD]


def part_copies(pos, parts, outs, sem):
    own, fwd, rev, far = outs
    c = pos[3]
    pairs = (
        (parts.at[2], far),
        (parts.at[3 - 2 * c], rev),
        (parts.at[1 + 2 * c], fwd),
        (parts.at[0], own),
    )
    return [pltpu.make_async_copy(src, dst, sem.at[n]) for n, (src, dst) in enumerate(pairs)]


PART_OUTS = (PAIR,) * 4


def bundle_kernel(
    base, pos, ids, pids, row_sources, before_in, weights, arrays, terms_out, own_out, par_out, part_outs, rows_out,
    rows, weight, amat, kv, grad, heads, terms, parts, row_sem, w_sem, q_sem, sem, part_sem, before,
):
    copies = []
    if base:
        fetch_rows(pos, ids, pids, row_sources, rows, row_sem)
    else:
        for s in range(SLOTS):
            pltpu.make_async_copy(row_sources[0].at[s], rows.at[s], row_sem.at[s]).start()
        before_copy = pltpu.make_async_copy(before_in, before, sem.at[4])
        before_copy.start()
    fetch_weights(pos, *weights, weight, w_sem)
    fetch_heads(pos, base, arrays, amat, q_sem)
    for s in range(SLOTS):
        pltpu.make_async_copy(rows.at[s], rows.at[s], row_sem.at[s]).wait()
    if base:
        copies.append(pltpu.make_async_copy(rows, rows_out, sem.at[0]))
        copies[-1].start()
    bundle_math(ids, pids, rows, weight, w_sem, amat, kv, grad, heads, q_sem)
    for n, out in enumerate((own_out, par_out)):
        copies.append(pltpu.make_async_copy(heads.at[n], out, sem.at[1 + n]))
        copies[-1].start()
    if base:
        weight_products(pos, grad, rows, parts)
        outs = part_copies(pos, parts, part_outs, part_sem)
        for copy in outs:
            copy.start()
        back_terms(grad, weight, terms, terms_out, sem.at[3])
    else:
        before_copy.wait()
        back_terms(grad, weight, terms, terms_out, sem.at[3], before)
    copies.append(pltpu.make_async_copy(terms, terms_out, sem.at[3]))
    if not base:
        weight_products(pos, grad, rows, parts)
        outs = part_copies(pos, parts, part_outs, part_sem)
        for copy in outs:
            copy.start()
    for copy in copies + outs:
        copy.wait()


def first_kernel(pos, ids, pids, *refs):
    sources, weights, arrays, refs = refs[:8], refs[8:12], refs[12:14], refs[14:]
    rows_out, terms_out, own_out, par_out, refs = *refs[:4], refs[4:]
    part_outs, refs = refs[:4], refs[4:]
    bundle_kernel(
        2, pos, ids, pids, sources, None, weights, arrays, terms_out, own_out, par_out, part_outs, rows_out, *refs, None
    )


def second_kernel(pos, ids, pids, *refs):
    sources, before_in, weights, arrays, refs = refs[:1], refs[1], refs[2:6], refs[6:8], refs[8:]
    terms_out, own_out, par_out, refs = *refs[:3], refs[3:]
    part_outs, refs = refs[:4], refs[4:]
    bundle_kernel(
        0, pos, ids, pids, sources, before_in, weights, arrays, terms_out, own_out, par_out, part_outs, None, *refs
    )


def bundle(kernel, name, out_shape, extra, pos, ids, pids, *arrays):
    return pl.pallas_call(
        kernel,
        out_shape=out_shape,
        grid_spec=pltpu.PrefetchScalarGridSpec(
            num_scalar_prefetch=3,
            grid=(),
            in_specs=[HBM] * len(arrays),
            out_specs=[HBM] * len(out_shape),
            scratch_shapes=[
                scratch((SLOTS, NBL, ENC_D)),
                scratch((2, 4, HD, ENC_D)),
                scratch((4, 4, 128, 256)),
                scratch((2, TOKENS, 512)),
                scratch((TOKENS, 1024)),
                scratch((2, 2, 4, 128, HD)),
                scratch((SLOTS, NBL, ENC_D)),
                scratch((4, 2, HD, ENC_D)),
                pltpu.SemaphoreType.DMA((SLOTS,)),
                pltpu.SemaphoreType.DMA((2,)),
                pltpu.SemaphoreType.DMA,
                pltpu.SemaphoreType.DMA((5,)),
                pltpu.SemaphoreType.DMA((4,)),
            ] + extra,
        ),
        compiler_params=params(60),
        cost_estimate=pl.CostEstimate(flops=6_000_000_000, bytes_accessed=16_000_000, transcendentals=300_000),
        name=name,
    )(pos, ids, pids, *arrays)


def first(*args):
    return bundle(first_kernel, "first_heads", (ROWS, ROWS, HEAD_OUT, HEAD_OUT) + PART_OUTS, [], *args)


def second(*args):
    return bundle(
        second_kernel, "second_heads", (ROWS, HEAD_OUT, HEAD_OUT) + PART_OUTS, [scratch((SLOTS, NBL, ENC_D))], *args
    )


def near_kernel(pos, *refs):
    values, outs = refs[:4], refs[4:]
    c = pos[3]
    for j in range(2):
        total = values[0][j].astype(F32)
        for value in values[1:]:
            total = total + value[j].astype(F32)
        total = total.astype(BF)
        low, high = total[:64], total[64:]
        outs[j][...] = jnp.where(c == 0, low, high)
        outs[2 + j][...] = jnp.where(c == 0, high, low)


def near_halves(pos, *values):
    return pl.pallas_call(
        near_kernel,
        out_shape=(SDS((64, ENC_D), BF),) * 4,
        grid_spec=pltpu.PrefetchScalarGridSpec(
            num_scalar_prefetch=1, grid=(), in_specs=[VMEM] * 4, out_specs=[VMEM] * 4
        ),
        compiler_params=params(16),
        cost_estimate=pl.CostEstimate(flops=1_000_000, bytes_accessed=2_500_000, transcendentals=0),
        name="near_halves",
    )(pos, *values)


def route_kernel(pos, ids, pids, terms, p_terms, own, fwd, rev, far, total):
    y, c = pos[1], pos[3]
    total[...] = jnp.zeros_like(total)
    for s in range(SLOTS):
        src = ids if s < 4 else pids
        owner, row = src[s % 4], src[4 + s % 4]

        @pl.when(lax.rem(owner, 2) == c)
        def _():
            place = lax.rem(owner // 2 + NY - y, NY) * 4 + row
            total[place] = total[place] + (terms[s].astype(F32) + p_terms[s ^ 4].astype(F32))

    far[...] = total[8:12].astype(BF)
    rev[...] = total[pl.ds(12 - 8 * c, 4)].astype(BF)
    fwd[...] = total[pl.ds(4 + 8 * c, 4)].astype(BF)
    own[...] = total[0:4].astype(BF)


def route(pos, ids, pids, terms, p_terms):
    return pl.pallas_call(
        route_kernel,
        out_shape=(SDS((4, NBL, ENC_D), BF),) * 4,
        grid_spec=pltpu.PrefetchScalarGridSpec(
            num_scalar_prefetch=3,
            grid=(),
            in_specs=[VMEM] * 2,
            out_specs=[VMEM] * 4,
            scratch_shapes=[scratch((16, NBL, ENC_D), F32)],
        ),
        compiler_params=params(40),
        cost_estimate=pl.CostEstimate(flops=10_000_000, bytes_accessed=8_000_000, transcendentals=0),
        name="route",
    )(pos, ids, pids, terms, p_terms)


def join_kernel(pos, own_a, own_b, got_a, got_b, att_out, dq_out):
    z, c = pos[2], pos[3]
    for j in range(4):
        for core, (a, b) in ((c, (own_a, own_b)), (1 - c, (got_a, got_b))):
            src = b if j < 2 else a
            col = column_of(z, core, j)
            for hi in range(2):
                lanes = pl.ds(pl.multiple_of((hi * NZ + col) * HD, HD), HD)
                att_out[:, lanes] = src[0, 2 * (j % 2) + hi]
                dq_out[:, lanes] = src[1, 2 * (j % 2) + hi]


def join(pos, *arrays):
    return pl.pallas_call(
        join_kernel,
        out_shape=(SDS((128, HQ), BF),) * 2,
        grid_spec=pltpu.PrefetchScalarGridSpec(
            num_scalar_prefetch=1, grid=(), in_specs=[VMEM] * 4, out_specs=[VMEM] * 2
        ),
        compiler_params=params(16),
        cost_estimate=pl.CostEstimate(flops=0, bytes_accessed=4_000_000, transcendentals=0),
        name="join",
    )(pos, *arrays)


def add(*values):
    total = values[0].astype(F32)
    for value in values[1:]:
        total = total + value.astype(F32)
    return total


def tie(*values):
    return lax.optimization_barrier(values)


def on_device(queries, encodings, weight, shard, row, pad, cotangent):
    dp, ctx = lax.axis_index("dp"), lax.axis_index("ctx")
    pos = jnp.stack([dp // NZ, ctx // 2, dp % NZ, ctx % 2]).astype(jnp.int32)
    core = ctx % 2
    ids = jnp.concatenate([shard.reshape(4), row.reshape(4), pad.reshape(4)])
    q = queries.reshape(128, HQ)
    cot = cotangent.reshape(128, HQ)
    enc = encodings.reshape(4, NBL, ENC_D)

    y1, y2, p_own, pids = send(enc, Y_FWD), send(enc, Y_REV), send(enc, SWAP), send(ids, SWAP)
    u3, u2 = send(weight, Z_OUT[3]), send(weight, Z_OUT[2])
    ua = jnp.stack([u2, u3])
    ua, y1, y2, p_own, pids, weight_2 = tie(ua, y1, y2, p_own, pids, weight)
    a1, a2, y3 = send(ua, X_FWD), send(ua, X_REV), send(y1, Y_FWD)
    u1, u0 = send(weight_2, Z_OUT[1]), send(weight_2, Z_OUT[0])
    ub = jnp.stack([u0, u1])
    heads_in = jnp.stack([q, cot]).reshape(2, 2, GROUP, HQ)
    a1, a2, y3, ub, y1, y2, heads_in = tie(a1, a2, y3, ub, y1, y2, heads_in)
    a3, heads_par = send(a1, X_FWD), send(heads_in, SWAP)
    p_y1, p_y2, p_y3 = send(y1, SWAP), send(y2, SWAP), send(y3, SWAP)
    a3, p_y1, p_y2, p_y3, heads_par, ub = tie(a3, p_y1, p_y2, p_y3, heads_par, ub)
    b1, b2, b3 = send(ub, X_FWD), send(ub, X_REV), send(ub, X_TWO)

    rows, terms_a, own_a, par_a, *parts_a = first(
        pos, ids, pids, enc, y1, y2, y3, p_own, p_y1, p_y2, p_y3, ua, a1, a2, a3, heads_in, heads_par
    )
    got_a = send(par_a, SWAP)
    ga_own, ga_fwd, ga_rev, ga_far = parts_a
    ga1, ga2 = send(ga_far, X_FWD), send(ga_rev, X_REV)
    terms, own_b, par_b, gb_own, gb_fwd, gb_rev, gb_far = second(
        pos, ids, pids, rows, terms_a, ub, b1, b2, b3, heads_in, heads_par
    )
    terms, ga1, ga2, got_a = tie(terms, ga1, ga2, got_a)
    p_terms = send(terms, SWAP)
    ga3 = send(add(ga_fwd, ga1).astype(BF), X_FWD)
    gb1 = send(gb_far, X_FWD)
    e_own, e_fwd, e_rev, e_far = route(pos, ids, pids, terms, p_terms)
    e1 = send(e_far, Y_FWD)
    ga3, gb1, gb_rev, _ = tie(ga3, gb1, gb_rev, e_far)
    far = send(add(ga_own, ga2, ga3).astype(BF), Z_PAIR_BACK)
    gb3 = send(add(gb_fwd, gb1).astype(BF), X_FWD)
    gb2 = send(gb_rev, X_REV)
    e2 = send(e_rev, Y_REV)
    gb2, gb3, far, e1, e2 = tie(gb2, gb3, far, e1, e2)
    e3 = send(add(e_fwd, e1).astype(BF), Y_FWD)
    s0, s1, t0, t1 = near_halves(pos, gb_own, gb2, gb3, far)
    s0, s1 = send(s0, Z_BACK[0]), send(s1, Z_BACK[1])
    t0, t1 = send(t0, Z_BACK_ACROSS[0]), send(t1, Z_BACK_ACROSS[1])
    s0, s1, t0, t1, par_b, e3 = tie(s0, s1, t0, t1, par_b, e3)
    half = add(s0, s1, t0, t1).astype(BF)
    got_b = send(par_b, SWAP)
    half = add(half, send(half, Y_UP), send(half, Y_DN), send(half, Y_TWO))
    rest = send(half, SWAP)
    low = jnp.where(core == 0, half, rest)
    high = jnp.where(core == 0, rest, half)
    weight_gradient = jnp.concatenate([low, high])

    enc_grad = add(e_own, e2, e3).astype(BF)
    att, dq = join(pos, own_a, own_b, got_a, got_b)
    return (
        att.reshape(1, 128, HQ),
        dq.reshape(1, 128, HQ),
        enc_grad.reshape(1, 4, NBL, ENC_D),
        weight_gradient,
    )


def solution(mesh):
    rows = P("dp", "ctx", None)
    return jax.shard_map(
        on_device,
        mesh=mesh,
        in_specs=(rows, P("dp", "ctx", None, None), P("dp", None), rows, rows, rows, rows),
        out_specs=(rows, rows, P("dp", "ctx", None, None), P("dp", None)),
        check_vma=False,
    )
```

```python
import functools

import jax
import jax.numpy as jnp
from jax import lax
from jax.experimental import pallas as pl
from jax.experimental.pallas import tpu as pltpu
from jax.sharding import PartitionSpec as P

HEADS = 16
HD = 128
ENC_D = 896
NBL = 128
GROUP = 64
HQ = 2048
NX, NY, NZ = 4, 4, 8
SLOTS = 8
NEG = -1e30
BF = jnp.bfloat16
F32 = jnp.float32
AXES = ("dp", "ctx")


def _lin(x, y, z, c):
    return ((x % NX) * NZ + z % NZ) * (NY * 2) + (y % NY) * 2 + c


def _pairs(move):
    return [
        (_lin(x, y, z, c), _lin(*move(x, y, z, c)))
        for x in range(NX)
        for z in range(NZ)
        for y in range(NY)
        for c in range(2)
    ]


Y_UP = _pairs(lambda x, y, z, c: (x, y + 1, z, c))
Y_DN = _pairs(lambda x, y, z, c: (x, y - 1, z, c))
Y_TWO = _pairs(lambda x, y, z, c: (x, y + 2, z, c))
Y_FWD = _pairs(lambda x, y, z, c: (x, y + 1 - 2 * c, z, c))
Y_REV = _pairs(lambda x, y, z, c: (x, y - 1 + 2 * c, z, c))
X_FWD = _pairs(lambda x, y, z, c: (x + 1 - 2 * c, y, z, c))
X_REV = _pairs(lambda x, y, z, c: (x - 1 + 2 * c, y, z, c))
X_TWO = _pairs(lambda x, y, z, c: (x + 2, y, z, c))
SWAP = _pairs(lambda x, y, z, c: (x, y, z, 1 - c))
Z_OUT = [_pairs(lambda x, y, z, c, j=j: (x, y, z + j if c == 0 else z - 1 - j, c)) for j in range(4)]
Z_BACK = [_pairs(lambda x, y, z, c, j=j: (x, y, z - j if c == 0 else z + 1 + j, c)) for j in range(2)]
Z_BACK_ACROSS = [
    _pairs(lambda x, y, z, c, j=j: (x, y, z - j if c == 0 else z + 1 + j, 1 - c)) for j in range(2)
]
Z_PAIR_BACK = _pairs(lambda x, y, z, c: (x, y, z - 2 + 4 * c, c))


def send(value, pairs):
    return lax.ppermute(value, AXES, pairs)


def column_of(z, c, j):
    return lax.rem(jnp.where(c == 0, z + NZ - j, z + 1 + j), NZ)


HBM = pl.BlockSpec(memory_space=pltpu.HBM)
VMEM = pl.BlockSpec(memory_space=pltpu.VMEM)
SDS = jax.ShapeDtypeStruct
PAIR = SDS((2, HD, ENC_D), BF)
SOLO = SDS((1, HD, ENC_D), BF)
ROWS = SDS((SLOTS, NBL, ENC_D), BF)
HEAD_OUT = SDS((2, 4, 128, HD), BF)
TOKENS = SLOTS * NBL


def params(mib):
    return pltpu.CompilerParams(vmem_limit_bytes=mib * 1024 * 1024)


def dot(a, b, dims):
    return lax.dot_general(a, b, (dims, ((), ())), preferred_element_type=F32)


def scratch(shape, dtype=BF):
    return pltpu.VMEM(shape, dtype)


def slot_value(ids, pids, which, s):
    index = which * 4 + lax.rem(s, 4) if not isinstance(s, int) else which * 4 + s % 4
    return jnp.where(s < 4, ids[index], pids[index])


def fetch_rows(pos, ids, pids, sources, rows, sem):
    y, c = pos[1], pos[3]

    def fetch(s, carry):
        owner = slot_value(ids, pids, 0, s)
        row = slot_value(ids, pids, 1, s)
        away = lax.rem(owner // 2 + NY - y, NY)
        other = lax.rem(owner, 2) != c
        for side in range(2):
            here = other if side else jnp.logical_not(other)
            core = 1 - c if side else c
            own, fwd, rev, far = sources[4 * side:4 * side + 4]
            for place, buf in ((0, own), (3 - 2 * core, fwd), (1 + 2 * core, rev), (2, far)):
                @pl.when(jnp.logical_and(here, away == place))
                def _():
                    pltpu.make_async_copy(buf.at[row], rows.at[s], sem.at[s]).start()
        return carry

    lax.fori_loop(0, SLOTS, fetch, 0)


def fetch_weights(pos, own, fwd, rev, far, weight, sem):
    c = pos[3]
    for xx in range(NX):
        away = lax.rem(xx + NX - pos[0], NX)
        place = (xx % 2) * 2 + xx // 2
        for j in range(2):
            for value, src in ((0, own), (3 - 2 * c, fwd), (1 + 2 * c, rev), (2, far)):
                @pl.when(away == value)
                def _():
                    pltpu.make_async_copy(src.at[j], weight.at[j, place], sem.at[j]).start()


def fetch_heads(pos, first, arrays, amat, sem):
    amat[:, :, 0:GROUP, HD:] = jnp.zeros((4, 4, GROUP, HD), BF)
    amat[:, :, GROUP:, 0:HD] = jnp.zeros((4, 4, GROUP, HD), BF)
    for j in range(2):
        col = column_of(pos[2], pos[3], first + j)
        for hi in range(2):
            lanes = pl.ds(pl.multiple_of((hi * NZ + col) * HD, HD), HD)
            for part in range(2):
                for kind in range(2):
                    src = arrays[part].at[kind, :, :, lanes]
                    there = pl.ds(2 * part, 2), pl.ds(kind * GROUP, GROUP), pl.ds(kind * HD, HD)
                    pltpu.make_async_copy(src, amat.at[2 * j + hi, there[0], there[1], there[2]], sem).start()


def wait_heads(amat, sem):
    half = amat.at[:, :, 0:GROUP]
    pltpu.make_async_copy(half, half, sem).wait()


def bundle_math(ids, pids, rows, weight, w_sem, amat, kv, grad, heads, q_sem):
    scale = HD ** -0.5
    lane = lax.broadcasted_iota(jnp.int32, (GROUP, 2 * NBL), 1)
    live = []
    for g in range(4):
        live0 = NBL - slot_value(ids, pids, 2, 2 * g)
        live1 = NBL - slot_value(ids, pids, 2, 2 * g + 1)
        live.append(lane < jnp.where(lane < NBL, live0, live1 + NBL))
    for j in range(2):
        pltpu.make_async_copy(weight.at[j], weight.at[j], w_sem.at[j]).wait()
        enc = rows[...].reshape(TOKENS, ENC_D)
        kv[j] = dot(enc, weight[j].reshape(512, ENC_D), ((1,), (1,))).astype(BF)
    wait_heads(amat, q_sem)

    def begin(j, g, hi):
        both = kv[j, g * 256:(g + 1) * 256, hi * 256:(hi + 1) * 256]
        mat = amat[2 * j + hi, g]
        return both, mat, dot(mat, both, ((1,), (1,)))

    steps = [(j, g, hi) for j in range(2) for g in range(4) for hi in range(2)]
    ahead = begin(*steps[0])
    for n, (j, g, hi) in enumerate(steps):
        both, mat, sd = ahead
        if n + 1 < len(steps):
            ahead = begin(*steps[n + 1])
        s = jnp.where(live[g], sd[:GROUP] * scale, NEG)
        e = jnp.exp(s - jnp.max(s, axis=1, keepdims=True))
        p = e * (1.0 / jnp.sum(e, axis=1, keepdims=True))
        dp = sd[GROUP:]
        delta = jnp.sum(p * dp, axis=1, keepdims=True)
        ds = p * (dp - delta) * scale
        pm = jnp.concatenate([ds.astype(BF), p.astype(BF)], axis=0)
        out = dot(pm, both, ((1,), (0,)))
        spot = pl.ds((g % 2) * GROUP, GROUP)
        heads[g // 2, 0, 2 * j + hi, spot] = out[GROUP:, HD:].astype(BF)
        heads[g // 2, 1, 2 * j + hi, spot] = out[:GROUP, :HD].astype(BF)
        cols = j * 512 + hi * 256
        grad[g * 256:(g + 1) * 256, cols:cols + 256] = dot(pm, mat, ((0,), (0,))).astype(BF)


def back_terms(grad, weight, terms, terms_out, sem, before=None):
    for t in range(4):
        total = dot(grad[t * 256:(t + 1) * 256], weight[...].reshape(1024, ENC_D), ((1,), (0,)))
        if before is not None:
            total = total + before[2 * t:2 * t + 2].reshape(256, ENC_D).astype(F32)
        terms[2 * t:2 * t + 2] = total.astype(BF).reshape(2, NBL, ENC_D)
        here = pl.ds(2 * t, 2)
        pltpu.make_async_copy(terms.at[here], terms_out.at[here], sem).start()


def weight_products(pos, grad, rows, parts):
    for j in range(2):
        for hi in range(2):
            cols = j * 512 + hi * 256
            product = dot(
                grad[:, cols:cols + 256], rows[...].reshape(TOKENS, ENC_D), ((0,), (0,))
            ).astype(BF)
            for kind in range(2):
                away = lax.rem(2 * kind + hi + NX - pos[0], NX)
                parts[away, j] = product[kind * HD:(kind + 1) * HD]


def part_copies(pos, parts, outs, sem):
    own, fwd, rev, far = outs
    c = pos[3]
    pairs = (
        (parts.at[2], far),
        (parts.at[3 - 2 * c], rev),
        (parts.at[1 + 2 * c], fwd),
        (parts.at[0], own),
    )
    return [pltpu.make_async_copy(src, dst, sem.at[n]) for n, (src, dst) in enumerate(pairs)]


PART_OUTS = (PAIR,) * 4


def bundle_kernel(
    base, pos, ids, pids, row_sources, before_in, weights, arrays, terms_out, own_out, par_out, part_outs, rows_out,
    rows, weight, amat, kv, grad, heads, terms, parts, row_sem, w_sem, q_sem, sem, part_sem, before,
):
    copies = []
    if base:
        fetch_rows(pos, ids, pids, row_sources, rows, row_sem)
    else:
        for s in range(SLOTS):
            pltpu.make_async_copy(row_sources[0].at[s], rows.at[s], row_sem.at[s]).start()
        before_copy = pltpu.make_async_copy(before_in, before, sem.at[4])
        before_copy.start()
    fetch_weights(pos, *weights, weight, w_sem)
    fetch_heads(pos, base, arrays, amat, q_sem)
    for s in range(SLOTS):
        pltpu.make_async_copy(rows.at[s], rows.at[s], row_sem.at[s]).wait()
    if base:
        copies.append(pltpu.make_async_copy(rows, rows_out, sem.at[0]))
        copies[-1].start()
    bundle_math(ids, pids, rows, weight, w_sem, amat, kv, grad, heads, q_sem)
    for n, out in enumerate((own_out, par_out)):
        copies.append(pltpu.make_async_copy(heads.at[n], out, sem.at[1 + n]))
        copies[-1].start()
    if base:
        weight_products(pos, grad, rows, parts)
        outs = part_copies(pos, parts, part_outs, part_sem)
        for copy in outs:
            copy.start()
        back_terms(grad, weight, terms, terms_out, sem.at[3])
    else:
        before_copy.wait()
        back_terms(grad, weight, terms, terms_out, sem.at[3], before)
    copies.append(pltpu.make_async_copy(terms, terms_out, sem.at[3]))
    if not base:
        weight_products(pos, grad, rows, parts)
        outs = part_copies(pos, parts, part_outs, part_sem)
        for copy in outs:
            copy.start()
    for copy in copies + outs:
        copy.wait()


def first_kernel(pos, ids, pids, *refs):
    sources, weights, arrays, refs = refs[:8], refs[8:12], refs[12:14], refs[14:]
    rows_out, terms_out, own_out, par_out, refs = *refs[:4], refs[4:]
    part_outs, refs = refs[:4], refs[4:]
    bundle_kernel(
        2, pos, ids, pids, sources, None, weights, arrays, terms_out, own_out, par_out, part_outs, rows_out, *refs, None
    )


def second_kernel(pos, ids, pids, *refs):
    sources, before_in, weights, arrays, refs = refs[:1], refs[1], refs[2:6], refs[6:8], refs[8:]
    terms_out, own_out, par_out, refs = *refs[:3], refs[3:]
    part_outs, refs = refs[:4], refs[4:]
    bundle_kernel(
        0, pos, ids, pids, sources, before_in, weights, arrays, terms_out, own_out, par_out, part_outs, None, *refs
    )


def bundle(kernel, name, out_shape, extra, pos, ids, pids, *arrays):
    return pl.pallas_call(
        kernel,
        out_shape=out_shape,
        grid_spec=pltpu.PrefetchScalarGridSpec(
            num_scalar_prefetch=3,
            grid=(),
            in_specs=[HBM] * len(arrays),
            out_specs=[HBM] * len(out_shape),
            scratch_shapes=[
                scratch((SLOTS, NBL, ENC_D)),
                scratch((2, 4, HD, ENC_D)),
                scratch((4, 4, 128, 256)),
                scratch((2, TOKENS, 512)),
                scratch((TOKENS, 1024)),
                scratch((2, 2, 4, 128, HD)),
                scratch((SLOTS, NBL, ENC_D)),
                scratch((4, 2, HD, ENC_D)),
                pltpu.SemaphoreType.DMA((SLOTS,)),
                pltpu.SemaphoreType.DMA((2,)),
                pltpu.SemaphoreType.DMA,
                pltpu.SemaphoreType.DMA((5,)),
                pltpu.SemaphoreType.DMA((4,)),
            ] + extra,
        ),
        compiler_params=params(60),
        cost_estimate=pl.CostEstimate(flops=6_000_000_000, bytes_accessed=16_000_000, transcendentals=300_000),
        name=name,
    )(pos, ids, pids, *arrays)


def first(*args):
    return bundle(first_kernel, "first_heads", (ROWS, ROWS, HEAD_OUT, HEAD_OUT) + PART_OUTS, [], *args)


def second(*args):
    return bundle(
        second_kernel, "second_heads", (ROWS, HEAD_OUT, HEAD_OUT) + PART_OUTS, [scratch((SLOTS, NBL, ENC_D))], *args
    )


def near_kernel(pos, *refs):
    values, outs = refs[:4], refs[4:]
    c = pos[3]
    for j in range(2):
        total = values[0][j].astype(F32)
        for value in values[1:]:
            total = total + value[j].astype(F32)
        total = total.astype(BF)
        low, high = total[:64], total[64:]
        outs[j][...] = jnp.where(c == 0, low, high)
        outs[2 + j][...] = jnp.where(c == 0, high, low)


def near_halves(pos, *values):
    return pl.pallas_call(
        near_kernel,
        out_shape=(SDS((64, ENC_D), BF),) * 4,
        grid_spec=pltpu.PrefetchScalarGridSpec(
            num_scalar_prefetch=1, grid=(), in_specs=[VMEM] * 4, out_specs=[VMEM] * 4
        ),
        compiler_params=params(16),
        cost_estimate=pl.CostEstimate(flops=1_000_000, bytes_accessed=2_500_000, transcendentals=0),
        name="near_halves",
    )(pos, *values)


def route_kernel(pos, ids, pids, terms, p_terms, own, fwd, rev, far, total):
    y, c = pos[1], pos[3]
    total[...] = jnp.zeros_like(total)
    for s in range(SLOTS):
        src = ids if s < 4 else pids
        owner, row = src[s % 4], src[4 + s % 4]

        @pl.when(lax.rem(owner, 2) == c)
        def _():
            place = lax.rem(owner // 2 + NY - y, NY) * 4 + row
            total[place] = total[place] + (terms[s].astype(F32) + p_terms[s ^ 4].astype(F32))

    far[...] = total[8:12].astype(BF)
    rev[...] = total[pl.ds(12 - 8 * c, 4)].astype(BF)
    fwd[...] = total[pl.ds(4 + 8 * c, 4)].astype(BF)
    own[...] = total[0:4].astype(BF)


def route(pos, ids, pids, terms, p_terms):
    return pl.pallas_call(
        route_kernel,
        out_shape=(SDS((4, NBL, ENC_D), BF),) * 4,
        grid_spec=pltpu.PrefetchScalarGridSpec(
            num_scalar_prefetch=3,
            grid=(),
            in_specs=[VMEM] * 2,
            out_specs=[VMEM] * 4,
            scratch_shapes=[scratch((16, NBL, ENC_D), F32)],
        ),
        compiler_params=params(40),
        cost_estimate=pl.CostEstimate(flops=10_000_000, bytes_accessed=8_000_000, transcendentals=0),
        name="route",
    )(pos, ids, pids, terms, p_terms)


def join_kernel(pos, own_a, own_b, got_a, got_b, att_out, dq_out):
    z, c = pos[2], pos[3]
    for j in range(4):
        for core, (a, b) in ((c, (own_a, own_b)), (1 - c, (got_a, got_b))):
            src = b if j < 2 else a
            col = column_of(z, core, j)
            for hi in range(2):
                lanes = pl.ds(pl.multiple_of((hi * NZ + col) * HD, HD), HD)
                att_out[:, lanes] = src[0, 2 * (j % 2) + hi]
                dq_out[:, lanes] = src[1, 2 * (j % 2) + hi]


def join(pos, *arrays):
    return pl.pallas_call(
        join_kernel,
        out_shape=(SDS((128, HQ), BF),) * 2,
        grid_spec=pltpu.PrefetchScalarGridSpec(
            num_scalar_prefetch=1, grid=(), in_specs=[VMEM] * 4, out_specs=[VMEM] * 2
        ),
        compiler_params=params(16),
        cost_estimate=pl.CostEstimate(flops=0, bytes_accessed=4_000_000, transcendentals=0),
        name="join",
    )(pos, *arrays)


def add(*values):
    total = values[0].astype(F32)
    for value in values[1:]:
        total = total + value.astype(F32)
    return total


def tie(*values):
    return lax.optimization_barrier(values)


def on_device(queries, encodings, weight, shard, row, pad, cotangent):
    dp, ctx = lax.axis_index("dp"), lax.axis_index("ctx")
    pos = jnp.stack([dp // NZ, ctx // 2, dp % NZ, ctx % 2]).astype(jnp.int32)
    core = ctx % 2
    ids = jnp.concatenate([shard.reshape(4), row.reshape(4), pad.reshape(4)])
    q = queries.reshape(128, HQ)
    cot = cotangent.reshape(128, HQ)
    enc = encodings.reshape(4, NBL, ENC_D)

    y1, y2, p_own, pids = send(enc, Y_FWD), send(enc, Y_REV), send(enc, SWAP), send(ids, SWAP)
    u3, u2 = send(weight, Z_OUT[3]), send(weight, Z_OUT[2])
    ua = jnp.stack([u2, u3])
    ua, y1, y2, p_own, pids, weight_2 = tie(ua, y1, y2, p_own, pids, weight)
    a1, a2, y3 = send(ua, X_FWD), send(ua, X_REV), send(y1, Y_FWD)
    u1, u0 = send(weight_2, Z_OUT[1]), send(weight_2, Z_OUT[0])
    ub = jnp.stack([u0, u1])
    heads_in = jnp.stack([q, cot]).reshape(2, 2, GROUP, HQ)
    a1, a2, y3, ub, y1, y2, heads_in = tie(a1, a2, y3, ub, y1, y2, heads_in)
    a3, heads_par = send(a1, X_FWD), send(heads_in, SWAP)
    p_y1, p_y2, p_y3 = send(y1, SWAP), send(y2, SWAP), send(y3, SWAP)
    a3, p_y1, p_y2, p_y3, heads_par, ub = tie(a3, p_y1, p_y2, p_y3, heads_par, ub)
    b1, b2, b3 = send(ub, X_FWD), send(ub, X_REV), send(ub, X_TWO)

    rows, terms_a, own_a, par_a, *parts_a = first(
        pos, ids, pids, enc, y1, y2, y3, p_own, p_y1, p_y2, p_y3, ua, a1, a2, a3, heads_in, heads_par
    )
    got_a = send(par_a, SWAP)
    ga_own, ga_fwd, ga_rev, ga_far = parts_a
    ga1, ga2 = send(ga_far, X_FWD), send(ga_rev, X_REV)
    terms, own_b, par_b, gb_own, gb_fwd, gb_rev, gb_far = second(
        pos, ids, pids, rows, terms_a, ub, b1, b2, b3, heads_in, heads_par
    )
    terms, ga1, ga2, got_a = tie(terms, ga1, ga2, got_a)
    p_terms = send(terms, SWAP)
    ga3 = send(add(ga_fwd, ga1).astype(BF), X_FWD)
    p_terms, ga3, gb_far, gb_rev = tie(p_terms, ga3, gb_far, gb_rev)
    far = send(add(ga_own, ga2, ga3).astype(BF), Z_PAIR_BACK)
    gb1, gb2 = send(gb_far, X_FWD), send(gb_rev, X_REV)
    e_own, e_fwd, e_rev, e_far = route(pos, ids, pids, terms, p_terms)
    e1, e2 = send(e_far, Y_FWD), send(e_rev, Y_REV)
    gb3 = send(add(gb_fwd, gb1).astype(BF), X_FWD)
    gb2, gb3, far, e1, e2 = tie(gb2, gb3, far, e1, e2)
    e3 = send(add(e_fwd, e1).astype(BF), Y_FWD)
    s0, s1, t0, t1 = near_halves(pos, gb_own, gb2, gb3, far)
    s0, s1 = send(s0, Z_BACK[0]), send(s1, Z_BACK[1])
    t0, t1 = send(t0, Z_BACK_ACROSS[0]), send(t1, Z_BACK_ACROSS[1])
    s0, s1, t0, t1, par_b, e3 = tie(s0, s1, t0, t1, par_b, e3)
    half = add(s0, s1, t0, t1).astype(BF)
    got_b = send(par_b, SWAP)
    half = add(half, send(half, Y_UP), send(half, Y_DN), send(half, Y_TWO))
    rest = send(half, SWAP)
    low = jnp.where(core == 0, half, rest)
    high = jnp.where(core == 0, rest, half)
    weight_gradient = jnp.concatenate([low, high])

    enc_grad = add(e_own, e2, e3).astype(BF)
    att, dq = join(pos, own_a, own_b, got_a, got_b)
    return (
        att.reshape(1, 128, HQ),
        dq.reshape(1, 128, HQ),
        enc_grad.reshape(1, 4, NBL, ENC_D),
        weight_gradient,
    )


def solution(mesh):
    rows = P("dp", "ctx", None)
    return jax.shard_map(
        on_device,
        mesh=mesh,
        in_specs=(rows, P("dp", "ctx", None, None), P("dp", None), rows, rows, rows, rows),
        out_specs=(rows, rows, P("dp", "ctx", None, None), P("dp", None)),
        check_vma=False,
    )
```
